256 devices in a mesh: space: 64 (over y, z, core), dp: 4 (over x).
Axes of the slice: x: 4, y: 4, z: 8, core: 2. Of those that a mesh axis runs over, the one named last changes fastest.
Arguments:
- inputs: bfloat16 [4, 64, 2, 16, 64, 128], P('dp', 'space'), may hold values from -6 to 6
- depth_one: bfloat16 [3, 3, 3, 128], replicated, may hold values from -1.25 to 1.25
- point_one: bfloat16 [128, 128], replicated, may hold values from -0.5 to 0.5
- depth_two: bfloat16 [3, 3, 3, 128], replicated, may hold values from -1.25 to 1.25
- point_two: bfloat16 [128, 128], replicated, may hold values from -0.5 to 0.5
- cotangent: bfloat16 [4, 64, 2, 16, 64, 128], P('dp', 'space'), may hold values from -6 to 6
Outputs:
- grad_input: bfloat16 [4, 64, 2, 16, 64, 128], P('dp', 'space')
- grad_depth_one: float32 [3, 3, 3, 128], replicated
- grad_point_one: float32 [128, 128], replicated
- grad_depth_two: float32 [3, 3, 3, 128], replicated
- grad_point_two: float32 [128, 128], replicated
The draws below stay inside these ranges and needn't reach their ends.
All inputs are finite; a program needn't handle non-finite values.
Results may differ from the reference program's by a relative error of at most 0.0068.
Values may be sent and summed in bfloat16 or wider, within the bound.
No kernel may reach another device: no remote copies, remote signals or barrier semaphores. Data moves between devices by JAX's collectives and lax.ppermute only.
A program may use at most 64 MiB of HBM per device.

```python
import math
import jax
import jax.numpy as jnp
from jax import lax

CH = 128
BX = 2
NY = 16
NZ = 64
NX = 128
SAMPLES = 4
N_SPACE = 64


def shard_levels(rng, dims, pieces, least, high):
    gain, own = 1.0, jax.random.fold_in(rng, 6)
    for position, shards_of in pieces:
        heights = jnp.exp(jax.random.uniform(jax.random.fold_in(own, position), (shards_of,), jnp.float32, least / len(pieces), high / len(pieces)))
        gain = gain * jnp.repeat(heights, dims[position] // shards_of).reshape([-1 if axis == position else 1 for axis in range(len(dims))])
    return gain


def normal_values(stream_key, shape, width, bound, pieces=(), dtype=jnp.bfloat16):
    entries = jax.random.normal(stream_key, shape, jnp.float32) * width
    if len(pieces) > 0:
        entries = shard_levels(stream_key, shape, pieces, -0.22, 0.18) * entries
    return jnp.clip(entries, min=-bound, max=bound).astype(dtype)


def setup_inputs(seed: int = 0) -> dict:
    key_of = jax.random.split(jax.random.key(seed), 7)
    inputs = normal_values(key_of[0], (SAMPLES, N_SPACE, BX, NY, NZ, CH), 1.0, 6.0, ((0, 4), (1, 64)))
    depth_one = normal_values(key_of[1], (3, 3, 3, CH), 27 ** -0.5, 1.25)
    point_one = normal_values(key_of[2], (CH, CH), CH ** -0.5, 0.5)
    depth_two = normal_values(key_of[3], (3, 3, 3, CH), 27 ** -0.5, 1.25)
    point_two = normal_values(key_of[4], (CH, CH), CH ** -0.5, 0.5)
    cotangent = normal_values(key_of[5], (SAMPLES, N_SPACE, BX, NY, NZ, CH), 1.0, 6.0, ((0, 4), (1, 64)))
    return dict(inputs=inputs, depth_one=depth_one, point_one=point_one, depth_two=depth_two, point_two=point_two, cotangent=cotangent)


def depthwise(volume, kernel):
    count = volume.shape[0] - 2
    wide_y = volume.shape[1]
    wide_z = volume.shape[2]
    padded = jnp.pad(volume.astype(jnp.float32), ((0, 0), (1, 1), (1, 1), (0, 0)))
    weights = kernel.astype(jnp.float32)
    total = jnp.zeros((count, wide_y, wide_z, volume.shape[3]), jnp.float32)
    for tap_x in range(3):
        for tap_y in range(3):
            for tap_z in range(3):
                total = total + padded[tap_x:tap_x + count, tap_y:tap_y + wide_y, tap_z:tap_z + wide_z] * weights[tap_x, tap_y, tap_z]
    return total

def depthwise_t(volume, kernel):
    count = volume.shape[0] - 2
    wide_y = volume.shape[1]
    wide_z = volume.shape[2]
    padded = jnp.pad(volume.astype(jnp.float32), ((0, 0), (1, 1), (1, 1), (0, 0)))
    weights = kernel.astype(jnp.float32)
    total = jnp.zeros((count, wide_y, wide_z, volume.shape[3]), jnp.float32)
    for tap_x in range(3):
        for tap_y in range(3):
            for tap_z in range(3):
                total = total + padded[2 - tap_x:2 - tap_x + count, 2 - tap_y:2 - tap_y + wide_y, 2 - tap_z:2 - tap_z + wide_z] * weights[tap_x, tap_y, tap_z]
    return total

def kernel_grad(volume, upstream):
    count = upstream.shape[0]
    wide_y = upstream.shape[1]
    wide_z = upstream.shape[2]
    padded = jnp.pad(volume.astype(jnp.float32), ((0, 0), (1, 1), (1, 1), (0, 0)))
    upper = upstream.astype(jnp.float32)
    rows = []
    for tap_x in range(3):
        for tap_y in range(3):
            for tap_z in range(3):
                rows.append(lax.optimization_barrier(jnp.sum(padded[tap_x:tap_x + count, tap_y:tap_y + wide_y, tap_z:tap_z + wide_z] * upper, axis=(0, 1, 2))))
    return jnp.stack(rows).reshape(3, 3, 3, upstream.shape[3])

def frame(volume):
    return jnp.pad(volume, ((1, 1), (0, 0), (0, 0), (0, 0)))

def silu_slope(value):
    sigma = jax.nn.sigmoid(value)
    return sigma * (1.0 + value * (1.0 - sigma))

def to_grid(blocks):
    channels = blocks.shape[5]
    return blocks.reshape(SAMPLES, NX, NY, NZ, channels)

def to_blocks(grid):
    channels = grid.shape[4]
    return grid.reshape(SAMPLES, N_SPACE, BX, NY, NZ, channels)

def reference(inputs, depth_one, point_one, depth_two, point_two, cotangent):
    channels = inputs.shape[5]
    grid_in = to_grid(inputs)
    grid_up = to_grid(cotangent)

    def one_sample(pair):
        sample, upstream = pair
        shape = sample.shape
        framed = frame(sample)
        mixed_one = depthwise(framed, depth_one).astype(jnp.bfloat16)
        pre_act = jnp.dot(mixed_one.reshape(-1, channels), point_one, preferred_element_type=jnp.float32)
        hidden = jax.nn.silu(pre_act).astype(jnp.bfloat16).reshape(shape)
        hidden_framed = frame(hidden)
        mixed_two = depthwise(hidden_framed, depth_two).astype(jnp.bfloat16)
        flat_up = upstream.reshape(-1, channels)
        g_point_two = jnp.dot(mixed_two.reshape(-1, channels).T, flat_up, preferred_element_type=jnp.float32)
        back_two = jnp.dot(flat_up, point_two.T, preferred_element_type=jnp.float32).astype(jnp.bfloat16).reshape(shape)
        g_depth_two = kernel_grad(hidden_framed, back_two)
        carried = depthwise_t(frame(back_two), depth_two)
        scaled = (carried.reshape(-1, channels) * silu_slope(pre_act)).astype(jnp.bfloat16)
        g_point_one = jnp.dot(mixed_one.reshape(-1, channels).T, scaled, preferred_element_type=jnp.float32)
        back_one = jnp.dot(scaled, point_one.T, preferred_element_type=jnp.float32).astype(jnp.bfloat16).reshape(shape)
        g_depth_one = kernel_grad(framed, back_one)
        grad_in = depthwise_t(frame(back_one), depth_one).astype(jnp.bfloat16)
        return (grad_in, g_depth_one, g_point_one, g_depth_two, g_point_two)
    grid_grad, g_d1, g_p1, g_d2, g_p2 = lax.map(one_sample, (grid_in, grid_up))
    factor = 1.0 / math.sqrt(SAMPLES * NX * NY * NZ)
    return (to_blocks(grid_grad), lax.optimization_barrier(jnp.sum(g_d1, axis=0)) * factor, lax.optimization_barrier(jnp.sum(g_p1, axis=0)) * factor, lax.optimization_barrier(jnp.sum(g_d2, axis=0)) * factor, lax.optimization_barrier(jnp.sum(g_p2, axis=0)) * factor)
```

```python
import functools
import math

import jax
import jax.numpy as jnp
from jax import lax
from jax.experimental import pallas as pl
from jax.experimental.pallas import tpu as pltpu
from jax.sharding import PartitionSpec as P

CH = 128
LINE = 64
CELLS = 1024
PADDED = CELLS + 2 * LINE
ROWS = 256
TERMS = 320
VMEM_LIMIT = 48 * 1024 * 1024


def mm(a, b):
    return jnp.dot(a, b, preferred_element_type=jnp.float32)


def keep_mask(count, edge):
    return lax.broadcasted_iota(jnp.int32, (count, 1), 0) % LINE != edge


def from_before(v):
    return jnp.where(keep_mask(v.shape[0], 0), pltpu.roll(v, 1, 0), 0.0)


def from_after(v):
    return jnp.where(keep_mask(v.shape[0], LINE - 1), pltpu.roll(v, v.shape[0] - 1, 0), 0.0)


def shift_sum(products, width):
    return (
        from_before(products[:, :width])
        + products[:, width : 2 * width]
        + from_after(products[:, 2 * width :])
    )


def set_plane(ref, slot, plane):
    edge = jnp.zeros((LINE, CH), jnp.bfloat16)
    ref[slot, 0:LINE, :] = edge
    ref[slot, LINE : LINE + CELLS, :] = plane
    ref[slot, LINE + CELLS : PADDED, :] = edge


def windows(ref, slots, start):
    return jnp.concatenate(
        [ref[p, start + b * LINE : start + b * LINE + ROWS, :] for p in slots for b in range(3)],
        axis=1,
    )


def fill_local(ref, tap_matrix):
    for p in range(2):
        for b in range(3):
            for e in range(3):
                for x in range(2):
                    row, col = ((p * 3 + b) * CH, (e * 2 + x) * CH)
                    ref[row : row + CH, col : col + CH] = tap_matrix(9 * (p + 1 - x) + 3 * b + e)


def fill_side(ref, tap_matrix):
    for b in range(3):
        for e in range(3):
            ref[b * CH : (b + 1) * CH, e * CH : (e + 1) * CH] = tap_matrix(3 * b + e)


def columns_of(depth):
    padded = jnp.concatenate([depth, jnp.zeros((CH - 27, CH), jnp.float32)], axis=0)
    return padded.T


def forward_taps(cols, point):
    return lambda s: (cols[:, s : s + 1] * point).astype(jnp.bfloat16)


def backward_taps(depth, point_t):
    return lambda s: (depth[26 - s : 27 - s, :] * point_t).astype(jnp.bfloat16)


def side_taps(matrix, high):
    def pick(j):
        return jnp.where(high, matrix(18 + j), matrix(j))

    return pick


def near_kernel(
    parity, block_in, block_up, near, d1, p1, d2, p2,
    pre, carried, far_w1, far_w2,
    planes_in, planes_up, w_local, w_side,
):
    core = parity[0]
    depth_one = d1[...].astype(jnp.float32)
    depth_two = d2[...].astype(jnp.float32)
    point_one = p1[...].astype(jnp.float32)
    point_two_t = p2[...].astype(jnp.float32).T
    taps_one = forward_taps(columns_of(depth_one), point_one)
    taps_two = backward_taps(depth_two, point_two_t)
    near_high = core == 0
    for which, planes, block, taps, out, far_w in (
        (0, planes_in, block_in, taps_one, pre, far_w1),
        (1, planes_up, block_up, taps_two, carried, far_w2),
    ):
        for x in range(2):
            set_plane(planes, x, block[x])
        set_plane(planes, 2, near[which])
        fill_local(w_local, taps)
        fill_side(w_side, side_taps(taps, near_high))
        fill_side(far_w, side_taps(taps, jnp.logical_not(near_high)))
        for start in range(0, CELLS, ROWS):
            both = shift_sum(mm(windows(planes, (0, 1), start), w_local[...]), 2 * CH)
            one = shift_sum(mm(windows(planes, (2,), start), w_side[...]), CH)
            out[0, start : start + ROWS, :] = both[:, :CH] + jnp.where(near_high, 0.0, one)
            out[1, start : start + ROWS, :] = both[:, CH:] + jnp.where(near_high, one, 0.0)


def tap_sums(left_t, planes, combine):
    order = [(a, b) for a in range(3) for b in range(3)]
    for at in range(0, 9, 2):
        group = order[at : at + 2]
        right = jnp.concatenate(
            [
                jnp.concatenate(
                    [planes[a + x, b * LINE : b * LINE + CELLS, :] for x in range(2)], axis=0
                )
                for a, b in group
            ],
            axis=1,
        )
        sums = mm(left_t[...], right)
        for i, (a, b) in enumerate(group):
            for e in range(3):
                combine(9 * a + 3 * b + e, sums[e * CH : (e + 1) * CH, i * CH : (i + 1) * CH])


def far_kernel(
    factor,
    parity, block_in, block_up, near, far, pre, carried, far_w1, far_w2, d1, p1, d2, p2,
    scaled_out, terms,
    planes_in, planes_up, scaled_t, hidden_t, total,
):
    core = parity[0]
    far_slot = 3 * core
    near_slot = 3 - far_slot
    for which, planes, block in ((0, planes_in, block_in), (1, planes_up, block_up)):
        for x in range(2):
            set_plane(planes, 1 + x, block[x])
        set_plane(planes, near_slot, near[which])
        set_plane(planes, far_slot, far[which])
    for start in range(0, CELLS, ROWS):
        more_pre = shift_sum(mm(windows(planes_in, (far_slot,), start), far_w1[...]), CH)
        more_carried = shift_sum(mm(windows(planes_up, (far_slot,), start), far_w2[...]), CH)
        for x in range(2):
            mine = core == x
            value = pre[x, start : start + ROWS, :] + jnp.where(mine, more_pre, 0.0)
            back = carried[x, start : start + ROWS, :] + jnp.where(mine, more_carried, 0.0)
            sigma = jax.nn.sigmoid(value)
            hidden = (value * sigma).astype(jnp.bfloat16).astype(jnp.float32)
            scaled = (back * (sigma * (1.0 + value * (1.0 - sigma)))).astype(jnp.bfloat16)
            scaled_out[x, start : start + ROWS, :] = scaled
            scaled = scaled.astype(jnp.float32)
            at = x * CELLS + start
            for ref, v in ((scaled_t, scaled), (hidden_t, hidden)):
                shifted = jnp.concatenate([from_after(v), v, from_before(v)], axis=1)
                ref[:, at : at + ROWS] = shifted.astype(jnp.bfloat16).T
    depth_one = d1[...].astype(jnp.float32)
    point_one_t = p1[...].astype(jnp.float32).T
    point_two = p2[...].astype(jnp.float32)
    cols_two = columns_of(d2[...].astype(jnp.float32))
    terms[...] = jnp.zeros((TERMS, CH), jnp.float32)
    total[...] = jnp.zeros((2, CH, CH), jnp.float32)
    lane = lax.broadcasted_iota(jnp.int32, (CH, CH), 1)

    def layer_one(s, block):
        total[0] += depth_one[s : s + 1, :] * block
        terms[s : s + 1, :] = jnp.sum(point_one_t * block, axis=0, keepdims=True) * factor

    tap_sums(scaled_t, planes_in, layer_one)
    terms[32:160, :] = total[0].T * factor
    total[0] = jnp.zeros((CH, CH), jnp.float32)

    def layer_two(s, block):
        s = 26 - s
        total[0] += cols_two[:, s : s + 1] * block
        total[1] += jnp.where(lane == s, jnp.sum(point_two * block, axis=1, keepdims=True), 0.0)

    tap_sums(hidden_t, planes_up, layer_two)
    terms[192:320, :] = total[0] * factor
    terms[160:192, :] = total[1].T[:32, :] * factor


def last_kernel(parity, scaled, near, far, d1, p1, out, planes, w_local, w_side):
    core = parity[0]
    depth_one = d1[...].astype(jnp.float32)
    taps = backward_taps(depth_one, p1[...].astype(jnp.float32).T)
    near_high = core == 0
    for x in range(2):
        set_plane(planes, x, scaled[x])
    set_plane(planes, 2, near[...])
    set_plane(planes, 3, far[...])
    fill_local(w_local, taps)
    for side, high in ((0, near_high), (1, jnp.logical_not(near_high))):
        w = w_side.at[side]
        fill_side(w, side_taps(taps, high))
    for start in range(0, CELLS, ROWS):
        both = shift_sum(mm(windows(planes, (0, 1), start), w_local[...]), 2 * CH)
        one = shift_sum(mm(windows(planes, (2,), start), w_side[0]), CH)
        two = shift_sum(mm(windows(planes, (3,), start), w_side[1]), CH)
        low = jnp.where(near_high, two, one)
        high = jnp.where(near_high, one, two)
        out[0, start : start + ROWS, :] = (both[:, :CH] + low).astype(jnp.bfloat16)
        out[1, start : start + ROWS, :] = (both[:, CH:] + high).astype(jnp.bfloat16)


def call(kernel, scratch, outs, flops, *args):
    vmem = pl.BlockSpec(memory_space=pltpu.VMEM)
    smem = pl.BlockSpec(memory_space=pltpu.SMEM)
    moved = sum(a.size * a.dtype.itemsize for a in args) + sum(
        o.size * o.dtype.itemsize for o in outs
    )
    return pl.pallas_call(
        kernel,
        out_shape=outs,
        in_specs=[smem] + [vmem] * (len(args) - 1),
        out_specs=[vmem] * len(outs),
        scratch_shapes=scratch,
        cost_estimate=pl.CostEstimate(flops=flops, bytes_accessed=moved, transcendentals=0),
        compiler_params=pltpu.CompilerParams(vmem_limit_bytes=VMEM_LIMIT),
    )(*args)


def swapped(near, far):
    count = lax.axis_size("space")
    pairs = [(i, i ^ 1) for i in range(count)]
    crossing = [(i, i + 1) for i in range(1, count - 1, 2)]
    crossing = crossing + [(j, i) for i, j in crossing]
    far = lax.ppermute(far, "space", crossing)
    near = lax.ppermute(near, "space", pairs)
    return near, far


def sum_of_terms(terms):
    count = lax.axis_size("space")
    tiles = terms.reshape(count, 1, -1)
    share = lax.all_to_all(tiles, "space", 0, 0, tiled=True).sum(axis=0)
    groups = lax.axis_size("dp")
    copies = jnp.broadcast_to(share, (groups, *share.shape))
    share = lax.all_to_all(copies, "dp", 0, 0, tiled=True).sum(axis=0)
    copies = jnp.broadcast_to(share, (count, *share.shape))
    return lax.all_to_all(copies, "space", 0, 0, tiled=True).reshape(TERMS, CH)


def on_device(inputs, depth_one, point_one, depth_two, point_two, cotangent):
    f32, bf16 = jnp.float32, jnp.bfloat16
    shape = jax.ShapeDtypeStruct
    block_in = inputs.reshape(2, CELLS, CH)
    block_up = cotangent.reshape(2, CELLS, CH)
    d1 = depth_one.reshape(27, CH)
    d2 = depth_two.reshape(27, CH)
    core = lax.axis_index("space") % 2
    parity = core.astype(jnp.int32).reshape(1)
    first = jnp.stack([block_in[0], block_up[0]])
    last = jnp.stack([block_in[1], block_up[1]])
    near, far = swapped(jnp.where(core == 0, last, first), jnp.where(core == 0, first, last))

    slots = pltpu.VMEM((4, PADDED, CH), bf16)
    local_w = pltpu.VMEM((6 * CH, 6 * CH), bf16)
    pre, carried, far_w1, far_w2 = call(
        near_kernel,
        [slots, slots, local_w, pltpu.VMEM((3 * CH, 3 * CH), bf16)],
        [shape((2, CELLS, CH), f32)] * 2 + [shape((3 * CH, 3 * CH), bf16)] * 2,
        4_000_000_000,
        parity, block_in, block_up, near, d1, point_one, d2, point_two,
    )
    cells = lax.axis_size("dp") * lax.axis_size("space") * 2 * CELLS
    scaled, terms = call(
        functools.partial(far_kernel, 1.0 / math.sqrt(cells)),
        [slots, slots] + [pltpu.VMEM((3 * CH, 2 * CELLS), bf16)] * 2 + [pltpu.VMEM((2, CH, CH), f32)],
        [shape((2, CELLS, CH), bf16), shape((TERMS, CH), f32)],
        4_000_000_000,
        parity, block_in, block_up, near, far, pre, carried, far_w1, far_w2,
        d1, point_one, d2, point_two,
    )
    near, far = swapped(
        jnp.where(core == 0, scaled[1], scaled[0]), jnp.where(core == 0, scaled[0], scaled[1])
    )
    (grad,) = call(
        last_kernel,
        [slots, local_w, pltpu.VMEM((2, 3 * CH, 3 * CH), bf16)],
        [shape((2, CELLS, CH), bf16)],
        4_000_000_000,
        parity, scaled, near, far, d1, point_one,
    )
    sums = sum_of_terms(terms)
    return (
        grad.reshape(inputs.shape),
        sums[:27].reshape(3, 3, 3, CH),
        sums[32:160],
        sums[160:187].reshape(3, 3, 3, CH),
        sums[192:320],
    )


def solution(mesh):
    slabs = P("dp", "space", None, None, None, None)
    return jax.shard_map(
        on_device,
        mesh=mesh,
        in_specs=(slabs, P(), P(), P(), P(), slabs),
        out_specs=(slabs, P(), P(), P(), P()),
        check_vma=False,
    )
```

```python
import functools
import math

import jax
import jax.numpy as jnp
from jax import lax
from jax.experimental import pallas as pl
from jax.experimental.pallas import tpu as pltpu
from jax.sharding import PartitionSpec as P

CH = 128
LINE = 64
CELLS = 1024
PADDED = CELLS + 2 * LINE
ROWS = 256
TERMS = 320
VMEM_LIMIT = 24 * 1024 * 1024


def mm(a, b):
    return jnp.dot(a, b, preferred_element_type=jnp.float32)


def keep_mask(count, edge):
    return lax.broadcasted_iota(jnp.int32, (count, 1), 0) % LINE != edge


def from_before(v):
    return jnp.where(keep_mask(v.shape[0], 0), pltpu.roll(v, 1, 0), 0.0)


def from_after(v):
    return jnp.where(keep_mask(v.shape[0], LINE - 1), pltpu.roll(v, v.shape[0] - 1, 0), 0.0)


def shift_sum(products, width):
    return (
        from_before(products[:, :width])
        + products[:, width : 2 * width]
        + from_after(products[:, 2 * width :])
    )


def set_plane(ref, slot, plane):
    edge = jnp.zeros((LINE, CH), jnp.bfloat16)
    ref[slot, 0:LINE, :] = edge
    ref[slot, LINE : LINE + CELLS, :] = plane
    ref[slot, LINE + CELLS : PADDED, :] = edge


def windows(ref, slot, count, start):
    return jnp.concatenate(
        [
            ref[slot + a, start + b * LINE : start + b * LINE + ROWS, :]
            for a in range(count)
            for b in range(3)
        ],
        axis=1,
    )


def fill_taps(ref, tap_matrix):
    for a in range(3):
        for b in range(3):
            for e in range(3):
                row, col = ((3 * a + b) * CH, e * CH)
                ref[row : row + CH, col : col + CH] = tap_matrix(9 * a + 3 * b + e)


def tap_rows(ref, a, count):
    return ref[pl.ds(pl.multiple_of(a * 3 * CH, CH), count * 3 * CH), :]


def columns_of(depth):
    padded = jnp.concatenate([depth, jnp.zeros((CH - 27, CH), jnp.float32)], axis=0)
    return padded.T


def forward_taps(cols, point):
    return lambda s: (cols[:, s : s + 1] * point).astype(jnp.bfloat16)


def backward_taps(depth, point_t):
    return lambda s: (depth[26 - s : 27 - s, :] * point_t).astype(jnp.bfloat16)


def tap_sums(left_t, planes, x, combine):
    order = [(a, b) for a in range(3) for b in range(3)]
    for at in range(0, 9, 2):
        group = order[at : at + 2]
        right = jnp.concatenate(
            [planes[x + a, b * LINE : b * LINE + CELLS, :] for a, b in group], axis=1
        )
        sums = mm(left_t[...], right)
        for i, (a, b) in enumerate(group):
            for e in range(3):
                combine(9 * a + 3 * b + e, sums[e * CH : (e + 1) * CH, i * CH : (i + 1) * CH])


def activate(value, back, scaled_out, scaled_t, hidden_t, start):
    sigma = jax.nn.sigmoid(value)
    hidden = (value * sigma).astype(jnp.bfloat16).astype(jnp.float32)
    scaled = (back * (sigma * (1.0 + value * (1.0 - sigma)))).astype(jnp.bfloat16)
    scaled_out[start : start + ROWS, :] = scaled
    scaled = scaled.astype(jnp.float32)
    for ref, v in ((scaled_t, scaled), (hidden_t, hidden)):
        shifted = jnp.concatenate([from_after(v), v, from_before(v)], axis=1)
        ref[:, start : start + ROWS] = shifted.astype(jnp.bfloat16).T


def weight_terms(factor, x, planes_in, planes_up, scaled_t, hidden_t, weights, total, before, terms):
    depth_one, point_one, depth_two, point_two = weights
    point_one_t = point_one.T
    cols_two = columns_of(depth_two)
    lane = lax.broadcasted_iota(jnp.int32, (CH, CH), 1)
    total[...] = jnp.zeros((3, CH, CH), jnp.float32)
    terms[...] = jnp.zeros((TERMS, CH), jnp.float32) if before is None else before[...]

    def layer_one(s, block):
        total[0] += depth_one[s : s + 1, :] * block
        terms[s : s + 1, :] += jnp.sum(point_one_t * block, axis=0, keepdims=True) * factor

    tap_sums(scaled_t, planes_in, x, layer_one)
    terms[32:160, :] += total[0].T * factor

    def layer_two(s, block):
        s = 26 - s
        total[1] += cols_two[:, s : s + 1] * block
        total[2] += jnp.where(lane == s, jnp.sum(point_two * block, axis=1, keepdims=True), 0.0)

    tap_sums(hidden_t, planes_up, x, layer_two)
    terms[192:320, :] += total[1] * factor
    terms[160:192, :] += total[2].T[:32, :] * factor


def place_planes(planes, block, core, near, far):
    for x in range(2):
        set_plane(planes, 1 + x, block[x])
    if near is not None:
        set_plane(planes, 3 - 3 * core, near)
    if far is not None:
        set_plane(planes, 3 * core, far)


def near_kernel(
    factor,
    parity, block_in, block_up, near, d1, p1, d2, p2,
    scaled_out, pre, carried, far_w1, far_w2, terms,
    planes_in, planes_up, w_one, w_two, scaled_t, hidden_t, total,
):
    core = parity[0]
    inner = 1 - core
    weights = tuple(w[...].astype(jnp.float32) for w in (d1, p1, d2, p2))
    depth_one, point_one, depth_two, point_two = weights
    place_planes(planes_in, block_in, core, near[0], None)
    place_planes(planes_up, block_up, core, near[1], None)
    fill_taps(w_one, forward_taps(columns_of(depth_one), point_one))
    fill_taps(w_two, backward_taps(depth_two, point_two.T))
    for start in range(0, CELLS, ROWS):
        value = shift_sum(mm(windows(planes_in, inner, 3, start), w_one[...]), CH)
        back = shift_sum(mm(windows(planes_up, inner, 3, start), w_two[...]), CH)
        activate(value, back, scaled_out, scaled_t, hidden_t, start)
    weight_terms(
        factor, inner, planes_in, planes_up, scaled_t, hidden_t, weights, total, None, terms
    )
    for planes, w, out, far_w in (
        (planes_in, w_one, pre, far_w1),
        (planes_up, w_two, carried, far_w2),
    ):
        far_w[...] = tap_rows(w, 2 * core, 1)
        for start in range(0, CELLS, ROWS):
            products = mm(windows(planes, 1, 2, start), tap_rows(w, 1 - core, 2))
            out[start : start + ROWS, :] = shift_sum(products, CH)


def far_kernel(
    factor,
    parity, block_in, block_up, far, pre, carried, far_w1, far_w2, d1, p1, d2, p2, before,
    scaled_out, terms,
    planes_in, planes_up, scaled_t, hidden_t, total,
):
    core = parity[0]
    weights = tuple(w[...].astype(jnp.float32) for w in (d1, p1, d2, p2))
    place_planes(planes_in, block_in, core, None, far[0])
    place_planes(planes_up, block_up, core, None, far[1])
    for start in range(0, CELLS, ROWS):
        value = shift_sum(mm(windows(planes_in, 3 * core, 1, start), far_w1[...]), CH)
        back = shift_sum(mm(windows(planes_up, 3 * core, 1, start), far_w2[...]), CH)
        value = value + pre[start : start + ROWS, :]
        back = back + carried[start : start + ROWS, :]
        activate(value, back, scaled_out, scaled_t, hidden_t, start)
    weight_terms(
        factor, core, planes_in, planes_up, scaled_t, hidden_t, weights, total, before, terms
    )


def last_kernel(parity, inner, outer, near, far, d1, p1, out, planes, w):
    core = parity[0]
    depth_one = d1[...].astype(jnp.float32)
    fill_taps(w, backward_taps(depth_one, p1[...].astype(jnp.float32).T))
    set_plane(planes, 2 - core, inner[...])
    set_plane(planes, 1 + core, outer[...])
    set_plane(planes, 3 - 3 * core, near[...])
    set_plane(planes, 3 * core, far[...])
    for x in range(2):
        for start in range(0, CELLS, ROWS):
            grad = shift_sum(mm(windows(planes, x, 3, start), w[...]), CH)
            out[x, start : start + ROWS, :] = grad.astype(jnp.bfloat16)


def parts_kernel(sums, depth_one, point_one, depth_two, point_two):
    for a in range(3):
        for b in range(3):
            row = 9 * a + 3 * b
            depth_one[a, b] = sums[row : row + 3, :]
            depth_two[a, b] = sums[160 + row : 163 + row, :]
    point_one[...] = sums[32:160, :]
    point_two[...] = sums[192:320, :]


def call(kernel, scratch, outs, flops, *args):
    vmem = pl.BlockSpec(memory_space=pltpu.VMEM)
    smem = pl.BlockSpec(memory_space=pltpu.SMEM)
    moved = sum(a.size * a.dtype.itemsize for a in args) + sum(
        o.size * o.dtype.itemsize for o in outs
    )
    return pl.pallas_call(
        kernel,
        out_shape=outs,
        in_specs=[smem if a.dtype == jnp.int32 else vmem for a in args],
        out_specs=[vmem] * len(outs),
        scratch_shapes=scratch,
        cost_estimate=pl.CostEstimate(flops=flops, bytes_accessed=moved, transcendentals=0),
        compiler_params=pltpu.CompilerParams(vmem_limit_bytes=VMEM_LIMIT),
    )(*args)


SPACE = ("outer", "ring", "core")
ACROSS = ("outer", "core", "dp")


def with_other_core(v):
    return lax.ppermute(v, "core", [(0, 1), (1, 0)])


def with_other_chip(v):
    count = math.prod(lax.axis_size(name) for name in SPACE)
    pairs = [(i, i + 1) for i in range(1, count - 1, 2)]
    return lax.ppermute(v, SPACE, pairs + [(j, i) for i, j in pairs])


def sum_of_terms(terms):
    count = math.prod(lax.axis_size(name) for name in ACROSS)
    tiles = terms.reshape(count, 1, -1)
    share = lax.all_to_all(tiles, ACROSS, 0, 0, tiled=True).sum(axis=0)
    copies = jnp.broadcast_to(share, (lax.axis_size("ring"), *share.shape))
    share = lax.all_to_all(copies, "ring", 0, 0, tiled=True).sum(axis=0)
    copies = jnp.broadcast_to(share, (count, *share.shape))
    return lax.all_to_all(copies, ACROSS, 0, 0, tiled=True).reshape(TERMS, CH)


def on_device(inputs, depth_one, point_one, depth_two, point_two, cotangent):
    f32, bf16 = jnp.float32, jnp.bfloat16
    shape = jax.ShapeDtypeStruct
    block_in = inputs.reshape(2, CELLS, CH)
    block_up = cotangent.reshape(2, CELLS, CH)
    d1 = depth_one.reshape(27, CH)
    d2 = depth_two.reshape(27, CH)
    core = lax.axis_index("core")
    parity = core.astype(jnp.int32).reshape(1)

    def both(x):
        return jnp.concatenate(
            [lax.dynamic_slice_in_dim(block, x, 1, 0) for block in (block_in, block_up)], axis=0
        )

    far = with_other_chip(both(core))
    near = with_other_core(both(1 - core))
    slots = pltpu.VMEM((4, PADDED, CH), bf16)
    taps_w = pltpu.VMEM((9 * CH, 3 * CH), bf16)
    flipped = pltpu.VMEM((3 * CH, CELLS), bf16)
    totals = pltpu.VMEM((3, CH, CH), f32)
    devices = math.prod(lax.axis_size(name) for name in ("dp", *SPACE))
    factor = 1.0 / math.sqrt(devices * 2 * CELLS)
    inner, pre, carried, far_w1, far_w2, terms = call(
        functools.partial(near_kernel, factor),
        [slots, slots, taps_w, taps_w, flipped, flipped, totals],
        [shape((CELLS, CH), bf16)]
        + [shape((CELLS, CH), f32)] * 2
        + [shape((3 * CH, 3 * CH), bf16)] * 2
        + [shape((TERMS, CH), f32)],
        8_000_000_000,
        parity, block_in, block_up, near, d1, point_one, d2, point_two,
    )
    inner_beside = with_other_core(inner)
    outer, terms = call(
        functools.partial(far_kernel, factor),
        [slots, slots, flipped, flipped, totals],
        [shape((CELLS, CH), bf16), shape((TERMS, CH), f32)],
        4_000_000_000,
        parity, block_in, block_up, far, pre, carried, far_w1, far_w2,
        d1, point_one, d2, point_two, terms,
    )
    outer_beside = with_other_chip(outer)
    (grad,) = call(
        last_kernel,
        [slots, taps_w],
        [shape((2, CELLS, CH), bf16)],
        4_000_000_000,
        parity, inner, outer, inner_beside, outer_beside, d1, point_one,
    )
    depth, point = (shape((3, 3, 3, CH), f32), shape((CH, CH), f32))
    parts = call(parts_kernel, [], [depth, point, depth, point], 0, sum_of_terms(terms))
    return (grad.reshape(inputs.shape), *parts)


def solution(mesh):
    count, samples = (mesh.shape["space"], mesh.shape["dp"])
    ring = min(8, count // 2)
    grid = mesh.devices.reshape(count // (2 * ring), ring, 2, samples)
    split = jax.sharding.Mesh(grid, (*SPACE, "dp"))
    slabs = P("dp", SPACE, None, None, None, None)
    return jax.shard_map(
        on_device,
        mesh=split,
        in_specs=(slabs, P(), P(), P(), P(), slabs),
        out_specs=(slabs, P(), P(), P(), P()),
        check_vma=False,
    )
```

```python
import functools
import math

import jax
import jax.numpy as jnp
from jax import lax
from jax.experimental import pallas as pl
from jax.experimental.pallas import tpu as pltpu
from jax.sharding import PartitionSpec as P

CH = 128
LINE = 64
CELLS = 1024
PADDED = CELLS + 2 * LINE
ROWS = 256
TERMS = 320
VMEM_LIMIT = 24 * 1024 * 1024


def mm(a, b):
    return jnp.dot(a, b, preferred_element_type=jnp.float32)


def keep_mask(count, edge):
    return lax.broadcasted_iota(jnp.int32, (count, 1), 0) % LINE != edge


def from_before(v):
    return jnp.where(keep_mask(v.shape[0], 0), pltpu.roll(v, 1, 0), 0.0)


def from_after(v):
    return jnp.where(keep_mask(v.shape[0], LINE - 1), pltpu.roll(v, v.shape[0] - 1, 0), 0.0)


def shift_sum(products, width):
    return (
        from_before(products[:, :width])
        + products[:, width : 2 * width]
        + from_after(products[:, 2 * width :])
    )


def set_plane(ref, slot, plane):
    edge = jnp.zeros((LINE, CH), jnp.bfloat16)
    ref[slot, 0:LINE, :] = edge
    ref[slot, LINE : LINE + CELLS, :] = plane
    ref[slot, LINE + CELLS : PADDED, :] = edge


def windows(ref, slot, count, start):
    return jnp.concatenate(
        [
            ref[slot + a, start + b * LINE : start + b * LINE + ROWS, :]
            for a in range(count)
            for b in range(3)
        ],
        axis=1,
    )


def fill_taps(ref, tap_matrix):
    for a in range(3):
        for b in range(3):
            for e in range(3):
                row, col = ((3 * a + b) * CH, e * CH)
                ref[row : row + CH, col : col + CH] = tap_matrix(9 * a + 3 * b + e)


def tap_rows(ref, a, count):
    return ref[pl.ds(pl.multiple_of(a * 3 * CH, CH), count * 3 * CH), :]


def columns_of(depth):
    padded = jnp.concatenate([depth, jnp.zeros((CH - 27, CH), jnp.float32)], axis=0)
    return padded.T


def forward_taps(cols, point):
    return lambda s: (cols[:, s : s + 1] * point).astype(jnp.bfloat16)


def backward_taps(depth, point_t):
    return lambda s: (depth[26 - s : 27 - s, :] * point_t).astype(jnp.bfloat16)


def tap_sums(left_t, planes, x, combine):
    order = [(a, b) for a in range(3) for b in range(3)]
    for at in range(0, 9, 2):
        group = order[at : at + 2]
        right = jnp.concatenate(
            [planes[x + a, b * LINE : b * LINE + CELLS, :] for a, b in group], axis=1
        )
        sums = mm(left_t[...], right)
        for i, (a, b) in enumerate(group):
            for e in range(3):
                combine(9 * a + 3 * b + e, sums[e * CH : (e + 1) * CH, i * CH : (i + 1) * CH])


def activate(value, back, scaled_out, scaled_t, hidden_t, start):
    sigma = jax.nn.sigmoid(value)
    hidden = (value * sigma).astype(jnp.bfloat16).astype(jnp.float32)
    scaled = (back * (sigma * (1.0 + value * (1.0 - sigma)))).astype(jnp.bfloat16)
    scaled_out[start : start + ROWS, :] = scaled
    scaled = scaled.astype(jnp.float32)
    for ref, v in ((scaled_t, scaled), (hidden_t, hidden)):
        shifted = jnp.concatenate([from_after(v), v, from_before(v)], axis=1)
        ref[:, start : start + ROWS] = shifted.astype(jnp.bfloat16).T


def weight_terms(factor, x, planes_in, planes_up, scaled_t, hidden_t, weights, total, before, terms):
    depth_one, point_one, depth_two, point_two = weights
    point_one_t = point_one.T
    cols_two = columns_of(depth_two)
    lane = lax.broadcasted_iota(jnp.int32, (CH, CH), 1)
    total[...] = jnp.zeros((3, CH, CH), jnp.float32)
    terms[...] = jnp.zeros((TERMS, CH), jnp.float32) if before is None else before[...]

    def layer_one(s, block):
        total[0] += depth_one[s : s + 1, :] * block
        terms[s : s + 1, :] += jnp.sum(point_one_t * block, axis=0, keepdims=True) * factor

    tap_sums(scaled_t, planes_in, x, layer_one)
    terms[32:160, :] += total[0].T * factor

    def layer_two(s, block):
        s = 26 - s
        total[1] += cols_two[:, s : s + 1] * block
        total[2] += jnp.where(lane == s, jnp.sum(point_two * block, axis=1, keepdims=True), 0.0)

    tap_sums(hidden_t, planes_up, x, layer_two)
    terms[192:320, :] += total[1] * factor
    terms[160:192, :] += total[2].T[:32, :] * factor


def place_planes(planes, block, core, near, far):
    for x in range(2):
        set_plane(planes, 1 + x, block[x])
    if near is not None:
        set_plane(planes, 3 - 3 * core, near)
    if far is not None:
        set_plane(planes, 3 * core, far)


def near_kernel(
    factor,
    parity, block_in, block_up, near, d1, p1, d2, p2,
    scaled_out, pre, carried, far_w1, far_w2, terms,
    planes_in, planes_up, w_one, w_two, scaled_t, hidden_t, total,
):
    core = parity[0]
    inner = 1 - core
    weights = tuple(w[...].astype(jnp.float32) for w in (d1, p1, d2, p2))
    depth_one, point_one, depth_two, point_two = weights
    place_planes(planes_in, block_in, core, near[0], None)
    place_planes(planes_up, block_up, core, near[1], None)
    fill_taps(w_one, forward_taps(columns_of(depth_one), point_one))
    fill_taps(w_two, backward_taps(depth_two, point_two.T))
    for start in range(0, CELLS, ROWS):
        value = shift_sum(mm(windows(planes_in, inner, 3, start), w_one[...]), CH)
        back = shift_sum(mm(windows(planes_up, inner, 3, start), w_two[...]), CH)
        activate(value, back, scaled_out, scaled_t, hidden_t, start)
    weight_terms(
        factor, inner, planes_in, planes_up, scaled_t, hidden_t, weights, total, None, terms
    )
    for planes, w, out, far_w in (
        (planes_in, w_one, pre, far_w1),
        (planes_up, w_two, carried, far_w2),
    ):
        far_w[...] = tap_rows(w, 2 * core, 1)
        for start in range(0, CELLS, ROWS):
            products = mm(windows(planes, 1, 2, start), tap_rows(w, 1 - core, 2))
            out[start : start + ROWS, :] = shift_sum(products, CH)


def far_kernel(
    factor,
    parity, block_in, block_up, far, pre, carried, far_w1, far_w2, d1, p1, d2, p2, before,
    scaled_out, terms,
    planes_in, planes_up, scaled_t, hidden_t, total,
):
    core = parity[0]
    weights = tuple(w[...].astype(jnp.float32) for w in (d1, p1, d2, p2))
    place_planes(planes_in, block_in, core, None, far[0])
    place_planes(planes_up, block_up, core, None, far[1])
    for start in range(0, CELLS, ROWS):
        value = shift_sum(mm(windows(planes_in, 3 * core, 1, start), far_w1[...]), CH)
        back = shift_sum(mm(windows(planes_up, 3 * core, 1, start), far_w2[...]), CH)
        value = value + pre[start : start + ROWS, :]
        back = back + carried[start : start + ROWS, :]
        activate(value, back, scaled_out, scaled_t, hidden_t, start)
    weight_terms(
        factor, core, planes_in, planes_up, scaled_t, hidden_t, weights, total, before, terms
    )


def last_kernel(parity, inner, outer, near, far, d1, p1, out, done, planes, w):
    core = parity[0]
    depth_one = d1[...].astype(jnp.float32)
    fill_taps(w, backward_taps(depth_one, p1[...].astype(jnp.float32).T))
    set_plane(planes, 2 - core, inner[...])
    set_plane(planes, 1 + core, outer[...])
    set_plane(planes, 3 - 3 * core, near[...])
    set_plane(planes, 3 * core, far[...])
    for x in range(2):
        for start in range(0, CELLS, ROWS):
            grad = shift_sum(mm(windows(planes, x, 3, start), w[...]), CH)
            out[x, start : start + ROWS, :] = grad.astype(jnp.bfloat16)
    done[...] = jnp.zeros((8, CH), jnp.float32)


def parts_kernel(sums, done, depth_one, point_one, depth_two, point_two):
    for a in range(3):
        for b in range(3):
            row = 9 * a + 3 * b
            depth_one[a, b] = sums[row : row + 3, :]
            depth_two[a, b] = sums[160 + row : 163 + row, :]
    point_one[...] = sums[32:160, :]
    point_two[...] = sums[192:320, :]


def call(kernel, scratch, outs, flops, *args):
    vmem = pl.BlockSpec(memory_space=pltpu.VMEM)
    smem = pl.BlockSpec(memory_space=pltpu.SMEM)
    moved = sum(a.size * a.dtype.itemsize for a in args) + sum(
        o.size * o.dtype.itemsize for o in outs
    )
    return pl.pallas_call(
        kernel,
        out_shape=outs,
        in_specs=[smem if a.dtype == jnp.int32 else vmem for a in args],
        out_specs=[vmem] * len(outs),
        scratch_shapes=scratch,
        cost_estimate=pl.CostEstimate(flops=flops, bytes_accessed=moved, transcendentals=0),
        compiler_params=pltpu.CompilerParams(vmem_limit_bytes=VMEM_LIMIT),
    )(*args)


SPACE = ("outer", "ring", "core")
ACROSS = ("outer", "core", "dp")


def with_other_core(v):
    return lax.ppermute(v, "core", [(0, 1), (1, 0)])


def with_other_chip(v):
    count = math.prod(lax.axis_size(name) for name in SPACE)
    pairs = [(i, i + 1) for i in range(1, count - 1, 2)]
    return lax.ppermute(v, SPACE, pairs + [(j, i) for i, j in pairs])


def reduced_across(terms):
    count = math.prod(lax.axis_size(name) for name in ACROSS)
    tiles = terms.reshape(count, 1, -1)
    return lax.all_to_all(tiles, ACROSS, 0, 0, tiled=True).sum(axis=0)


def reduced_around(share):
    copies = jnp.broadcast_to(share, (lax.axis_size("ring"), *share.shape))
    return lax.all_to_all(copies, "ring", 0, 0, tiled=True).sum(axis=0)


def gathered_across(share):
    count = math.prod(lax.axis_size(name) for name in ACROSS)
    copies = jnp.broadcast_to(share, (count, *share.shape))
    return lax.all_to_all(copies, ACROSS, 0, 0, tiled=True).reshape(TERMS, CH)


def on_device(inputs, depth_one, point_one, depth_two, point_two, cotangent):
    f32, bf16 = jnp.float32, jnp.bfloat16
    shape = jax.ShapeDtypeStruct
    block_in = inputs.reshape(2, CELLS, CH)
    block_up = cotangent.reshape(2, CELLS, CH)
    d1 = depth_one.reshape(27, CH)
    d2 = depth_two.reshape(27, CH)
    core = lax.axis_index("core")
    parity = core.astype(jnp.int32).reshape(1)


    def both(x):
        return jnp.concatenate(
            [lax.dynamic_slice_in_dim(block, x, 1, 0) for block in (block_in, block_up)], axis=0
        )

    far = with_other_chip(both(core))
    near = with_other_core(both(1 - core))
    slots = pltpu.VMEM((4, PADDED, CH), bf16)
    taps_w = pltpu.VMEM((9 * CH, 3 * CH), bf16)
    flipped = pltpu.VMEM((3 * CH, CELLS), bf16)
    totals = pltpu.VMEM((3, CH, CH), f32)
    devices = math.prod(lax.axis_size(name) for name in ("dp", *SPACE))
    factor = 1.0 / math.sqrt(devices * 2 * CELLS)
    inner, pre, carried, far_w1, far_w2, terms = call(
        functools.partial(near_kernel, factor),
        [slots, slots, taps_w, taps_w, flipped, flipped, totals],
        [shape((CELLS, CH), bf16)]
        + [shape((CELLS, CH), f32)] * 2
        + [shape((3 * CH, 3 * CH), bf16)] * 2
        + [shape((TERMS, CH), f32)],
        8_000_000_000,
        parity, block_in, block_up, near, d1, point_one, d2, point_two,
    )
    outer, terms = call(
        functools.partial(far_kernel, factor),
        [slots, slots, flipped, flipped, totals],
        [shape((CELLS, CH), bf16), shape((TERMS, CH), f32)],
        4_000_000_000,
        parity, block_in, block_up, far, pre, carried, far_w1, far_w2,
        d1, point_one, d2, point_two, terms,
    )
    share = reduced_across(terms)
    share, inner, outer = lax.optimization_barrier((share, inner, outer))
    outer_beside = with_other_chip(outer)
    inner_beside = with_other_core(inner)
    grad, done = call(
        last_kernel,
        [slots, taps_w],
        [shape((2, CELLS, CH), bf16), shape((8, CH), f32)],
        4_000_000_000,
        parity, inner, outer, inner_beside, outer_beside, d1, point_one,
    )
    sums = gathered_across(reduced_around(share))
    depth, point = (shape((3, 3, 3, CH), f32), shape((CH, CH), f32))
    parts = call(parts_kernel, [], [depth, point, depth, point], 0, sums, done)
    return (grad.reshape(inputs.shape), *parts)


def solution(mesh):
    count, samples = (mesh.shape["space"], mesh.shape["dp"])
    ring = min(8, count // 2)
    grid = mesh.devices.reshape(count // (2 * ring), ring, 2, samples)
    split = jax.sharding.Mesh(grid, (*SPACE, "dp"))
    slabs = P("dp", SPACE, None, None, None, None)
    return jax.shard_map(
        on_device,
        mesh=split,
        in_specs=(slabs, P(), P(), P(), P(), slabs),
        out_specs=(slabs, P(), P(), P(), P()),
        check_vma=False,
    )
```

```python
import functools
import math

import jax
import jax.numpy as jnp
from jax import lax
from jax.experimental import pallas as pl
from jax.experimental.pallas import tpu as pltpu
from jax.sharding import PartitionSpec as P

CH = 128
LINE = 64
CELLS = 1024
PADDED = CELLS + 2 * LINE
ROWS = 256
TERMS = 320
VMEM_LIMIT = 24 * 1024 * 1024


def mm(a, b):
    return jnp.dot(a, b, preferred_element_type=jnp.float32)


def keep_mask(count, edge):
    return lax.broadcasted_iota(jnp.int32, (count, 1), 0) % LINE != edge


def from_before(v):
    return jnp.where(keep_mask(v.shape[0], 0), pltpu.roll(v, 1, 0), 0.0)


def from_after(v):
    return jnp.where(keep_mask(v.shape[0], LINE - 1), pltpu.roll(v, v.shape[0] - 1, 0), 0.0)


def shift_sum(products, width):
    return (
        from_before(products[:, :width])
        + products[:, width : 2 * width]
        + from_after(products[:, 2 * width :])
    )


def set_plane(ref, slot, plane):
    edge = jnp.zeros((LINE, CH), jnp.bfloat16)
    ref[slot, 0:LINE, :] = edge
    ref[slot, LINE : LINE + CELLS, :] = plane
    ref[slot, LINE + CELLS : PADDED, :] = edge


def local_products(planes, weights, start):
    left = jnp.concatenate(
        [
            planes[1 + p, start + b * LINE : start + b * LINE + ROWS, :]
            for p in range(2)
            for b in range(3)
        ],
        axis=1,
    )
    return shift_sum(mm(left, weights[...]), 2 * CH)


def side_products(planes, slot, weights, start):
    pairs = ROWS // LINE
    left = jnp.concatenate(
        [
            jnp.concatenate(
                [
                    planes[slot, start + (2 * j + i) * LINE : start + (2 * j + i + 1) * LINE, :]
                    for j in range(pairs)
                ],
                axis=0,
            )
            for i in range(4)
        ],
        axis=1,
    )
    out = shift_sum(mm(left, weights[...]), 2 * CH)
    return jnp.concatenate(
        [
            out[j * LINE : (j + 1) * LINE, q * CH : (q + 1) * CH]
            for j in range(pairs)
            for q in range(2)
        ],
        axis=0,
    )


def fill_local(ref, tap_matrix):
    for a in range(3):
        for b in range(3):
            for e in range(3):
                block = tap_matrix(9 * a + 3 * b + e)
                for p in range(2):
                    x = p + 1 - a
                    if 0 <= x < 2:
                        row, col = ((3 * p + b) * CH, (2 * e + x) * CH)
                        ref[row : row + CH, col : col + CH] = block


def fill_side(ref, tap_matrix, high):
    ref[...] = jnp.zeros(ref.shape, jnp.bfloat16)
    for b in range(3):
        for e in range(3):
            block = jnp.where(high, tap_matrix(18 + 3 * b + e), tap_matrix(3 * b + e))
            for q in range(2):
                row, col = ((b + q) * CH, (2 * e + q) * CH)
                ref[row : row + CH, col : col + CH] = block


def columns_of(depth):
    padded = jnp.concatenate([depth, jnp.zeros((CH - 27, CH), jnp.float32)], axis=0)
    return padded.T


def forward_taps(cols, point):
    return lambda s: (cols[:, s : s + 1] * point).astype(jnp.bfloat16)


def backward_taps(depth, point_t):
    return lambda s: (depth[26 - s : 27 - s, :] * point_t).astype(jnp.bfloat16)


def tap_sums(left_t, planes, x, combine):
    order = [(a, b) for a in range(3) for b in range(3)]
    for at in range(0, 9, 2):
        group = order[at : at + 2]
        right = jnp.concatenate(
            [planes[x + a, b * LINE : b * LINE + CELLS, :] for a, b in group], axis=1
        )
        sums = mm(left_t[...], right)
        for i, (a, b) in enumerate(group):
            for e in range(3):
                combine(9 * a + 3 * b + e, sums[e * CH : (e + 1) * CH, i * CH : (i + 1) * CH])


def activate(value, back, scaled_out, scaled_t, hidden_t, start):
    sigma = jax.nn.sigmoid(value)
    hidden = (value * sigma).astype(jnp.bfloat16).astype(jnp.float32)
    scaled = (back * (sigma * (1.0 + value * (1.0 - sigma)))).astype(jnp.bfloat16)
    scaled_out[start : start + ROWS, :] = scaled
    scaled = scaled.astype(jnp.float32)
    for ref, v in ((scaled_t, scaled), (hidden_t, hidden)):
        shifted = jnp.concatenate([from_after(v), v, from_before(v)], axis=1)
        ref[:, start : start + ROWS] = shifted.astype(jnp.bfloat16).T


def weight_terms(factor, x, planes_in, planes_up, scaled_t, hidden_t, weights, total, before, terms):
    depth_one, point_one, depth_two, point_two = weights
    point_one_t = point_one.T
    cols_two = columns_of(depth_two)
    lane = lax.broadcasted_iota(jnp.int32, (CH, CH), 1)
    total[...] = jnp.zeros((3, CH, CH), jnp.float32)
    terms[...] = jnp.zeros((TERMS, CH), jnp.float32) if before is None else before[...]

    def layer_one(s, block):
        total[0] += depth_one[s : s + 1, :] * block
        terms[s : s + 1, :] += jnp.sum(point_one_t * block, axis=0, keepdims=True) * factor

    tap_sums(scaled_t, planes_in, x, layer_one)
    terms[32:160, :] += total[0].T * factor

    def layer_two(s, block):
        s = 26 - s
        total[1] += cols_two[:, s : s + 1] * block
        total[2] += jnp.where(lane == s, jnp.sum(point_two * block, axis=1, keepdims=True), 0.0)

    tap_sums(hidden_t, planes_up, x, layer_two)
    terms[192:320, :] += total[1] * factor
    terms[160:192, :] += total[2].T[:32, :] * factor


def place_planes(planes, block, core, near, far):
    for x in range(2):
        set_plane(planes, 1 + x, block[x])
    if near is not None:
        set_plane(planes, 3 - 3 * core, near)
    if far is not None:
        set_plane(planes, 3 * core, far)


def near_kernel(
    factor,
    parity, block_in, block_up, near, d1, p1, d2, p2,
    scaled_out, pre, carried, far_w1, far_w2, terms,
    planes_in, planes_up, local_one, local_two, side_one, side_two, scaled_t, hidden_t, total,
):
    core = parity[0]
    inner = 1 - core
    weights = tuple(w[...].astype(jnp.float32) for w in (d1, p1, d2, p2))
    depth_one, point_one, depth_two, point_two = weights
    place_planes(planes_in, block_in, core, near[0], None)
    place_planes(planes_up, block_up, core, near[1], None)
    near_high = core == 0
    taps_one = forward_taps(columns_of(depth_one), point_one)
    taps_two = backward_taps(depth_two, point_two.T)
    for taps, local, side, other in (
        (taps_one, local_one, side_one, far_w1),
        (taps_two, local_two, side_two, far_w2),
    ):
        fill_local(local, taps)
        fill_side(side, taps, near_high)
        fill_side(other, taps, jnp.logical_not(near_high))
    near_slot = 3 - 3 * core
    for half in range(0, CELLS, 2 * ROWS):
        side_in = side_products(planes_in, near_slot, side_one, half)
        side_up = side_products(planes_up, near_slot, side_two, half)
        for at in range(0, 2 * ROWS, ROWS):
            start = half + at
            both_in = local_products(planes_in, local_one, start)
            both_up = local_products(planes_up, local_two, start)
            low, high = (both_in[:, :CH], both_in[:, CH:])
            pre[start : start + ROWS, :] = jnp.where(near_high, low, high)
            value = jnp.where(near_high, high, low) + side_in[at : at + ROWS, :]
            low, high = (both_up[:, :CH], both_up[:, CH:])
            carried[start : start + ROWS, :] = jnp.where(near_high, low, high)
            back = jnp.where(near_high, high, low) + side_up[at : at + ROWS, :]
            activate(value, back, scaled_out, scaled_t, hidden_t, start)
    weight_terms(
        factor, inner, planes_in, planes_up, scaled_t, hidden_t, weights, total, None, terms
    )


def far_kernel(
    factor,
    parity, block_in, block_up, far, pre, carried, far_w1, far_w2, d1, p1, d2, p2, before,
    scaled_out, terms,
    planes_in, planes_up, scaled_t, hidden_t, total,
):
    core = parity[0]
    weights = tuple(w[...].astype(jnp.float32) for w in (d1, p1, d2, p2))
    place_planes(planes_in, block_in, core, None, far[0])
    place_planes(planes_up, block_up, core, None, far[1])
    for half in range(0, CELLS, 2 * ROWS):
        side_in = side_products(planes_in, 3 * core, far_w1, half)
        side_up = side_products(planes_up, 3 * core, far_w2, half)
        for at in range(0, 2 * ROWS, ROWS):
            start = half + at
            value = side_in[at : at + ROWS, :] + pre[start : start + ROWS, :]
            back = side_up[at : at + ROWS, :] + carried[start : start + ROWS, :]
            activate(value, back, scaled_out, scaled_t, hidden_t, start)
    weight_terms(
        factor, core, planes_in, planes_up, scaled_t, hidden_t, weights, total, before, terms
    )


def last_kernel(parity, inner, outer, near, far, d1, p1, out, done, planes, local, low_side, high_side):
    core = parity[0]
    depth_one = d1[...].astype(jnp.float32)
    taps = backward_taps(depth_one, p1[...].astype(jnp.float32).T)
    fill_local(local, taps)
    fill_side(low_side, taps, False)
    fill_side(high_side, taps, True)
    set_plane(planes, 2 - core, inner[...])
    set_plane(planes, 1 + core, outer[...])
    set_plane(planes, 3 - 3 * core, near[...])
    set_plane(planes, 3 * core, far[...])
    for half in range(0, CELLS, 2 * ROWS):
        low = side_products(planes, 0, low_side, half)
        high = side_products(planes, 3, high_side, half)
        for at in range(0, 2 * ROWS, ROWS):
            start = half + at
            both = local_products(planes, local, start)
            grad = both[:, :CH] + low[at : at + ROWS, :]
            out[0, start : start + ROWS, :] = grad.astype(jnp.bfloat16)
            grad = both[:, CH:] + high[at : at + ROWS, :]
            out[1, start : start + ROWS, :] = grad.astype(jnp.bfloat16)
    done[...] = jnp.zeros((8, CH), jnp.float32)


def parts_kernel(sums, done, depth_one, point_one, depth_two, point_two):
    for a in range(3):
        for b in range(3):
            row = 9 * a + 3 * b
            depth_one[a, b] = sums[row : row + 3, :]
            depth_two[a, b] = sums[160 + row : 163 + row, :]
    point_one[...] = sums[32:160, :]
    point_two[...] = sums[192:320, :]


def call(kernel, scratch, outs, flops, *args):
    vmem = pl.BlockSpec(memory_space=pltpu.VMEM)
    smem = pl.BlockSpec(memory_space=pltpu.SMEM)
    moved = sum(a.size * a.dtype.itemsize for a in args) + sum(
        o.size * o.dtype.itemsize for o in outs
    )
    return pl.pallas_call(
        kernel,
        out_shape=outs,
        in_specs=[smem if a.dtype == jnp.int32 else vmem for a in args],
        out_specs=[vmem] * len(outs),
        scratch_shapes=scratch,
        cost_estimate=pl.CostEstimate(flops=flops, bytes_accessed=moved, transcendentals=0),
        compiler_params=pltpu.CompilerParams(vmem_limit_bytes=VMEM_LIMIT),
    )(*args)


SPACE = ("outer", "ring", "core")
ACROSS = ("outer", "core", "dp")


def with_other_core(v):
    return lax.ppermute(v, "core", [(0, 1), (1, 0)])


def with_other_chip(v):
    count = math.prod(lax.axis_size(name) for name in SPACE)
    pairs = [(i, i + 1) for i in range(1, count - 1, 2)]
    return lax.ppermute(v, SPACE, pairs + [(j, i) for i, j in pairs])


def reduced_across(terms):
    count = math.prod(lax.axis_size(name) for name in ACROSS)
    tiles = terms.reshape(count, 1, -1)
    return lax.all_to_all(tiles, ACROSS, 0, 0, tiled=True).sum(axis=0)


def reduced_around(share):
    copies = jnp.broadcast_to(share, (lax.axis_size("ring"), *share.shape))
    return lax.all_to_all(copies, "ring", 0, 0, tiled=True).sum(axis=0)


def gathered_across(share):
    count = math.prod(lax.axis_size(name) for name in ACROSS)
    copies = jnp.broadcast_to(share, (count, *share.shape))
    return lax.all_to_all(copies, ACROSS, 0, 0, tiled=True).reshape(TERMS, CH)


def on_device(inputs, depth_one, point_one, depth_two, point_two, cotangent):
    f32, bf16 = jnp.float32, jnp.bfloat16
    shape = jax.ShapeDtypeStruct
    block_in = inputs.reshape(2, CELLS, CH)
    block_up = cotangent.reshape(2, CELLS, CH)
    d1 = depth_one.reshape(27, CH)
    d2 = depth_two.reshape(27, CH)
    core = lax.axis_index("core")
    parity = core.astype(jnp.int32).reshape(1)


    def both(x):
        return jnp.concatenate(
            [lax.dynamic_slice_in_dim(block, x, 1, 0) for block in (block_in, block_up)], axis=0
        )

    far = with_other_chip(both(core))
    near = with_other_core(both(1 - core))
    slots = pltpu.VMEM((4, PADDED, CH), bf16)
    local_w = pltpu.VMEM((6 * CH, 6 * CH), bf16)
    side_w = pltpu.VMEM((4 * CH, 6 * CH), bf16)
    flipped = pltpu.VMEM((3 * CH, CELLS), bf16)
    totals = pltpu.VMEM((3, CH, CH), f32)
    devices = math.prod(lax.axis_size(name) for name in ("dp", *SPACE))
    factor = 1.0 / math.sqrt(devices * 2 * CELLS)
    inner, pre, carried, far_w1, far_w2, terms = call(
        functools.partial(near_kernel, factor),
        [slots, slots, local_w, local_w, side_w, side_w, flipped, flipped, totals],
        [shape((CELLS, CH), bf16)]
        + [shape((CELLS, CH), f32)] * 2
        + [shape((4 * CH, 6 * CH), bf16)] * 2
        + [shape((TERMS, CH), f32)],
        8_000_000_000,
        parity, block_in, block_up, near, d1, point_one, d2, point_two,
    )
    outer, terms = call(
        functools.partial(far_kernel, factor),
        [slots, slots, flipped, flipped, totals],
        [shape((CELLS, CH), bf16), shape((TERMS, CH), f32)],
        4_000_000_000,
        parity, block_in, block_up, far, pre, carried, far_w1, far_w2,
        d1, point_one, d2, point_two, terms,
    )
    share = reduced_across(terms)
    outer_beside = with_other_chip(outer)
    inner_beside = with_other_core(inner)
    grad, done = call(
        last_kernel,
        [slots, local_w, side_w, side_w],
        [shape((2, CELLS, CH), bf16), shape((8, CH), f32)],
        4_000_000_000,
        parity, inner, outer, inner_beside, outer_beside, d1, point_one,
    )
    sums = gathered_across(reduced_around(share))
    depth, point = (shape((3, 3, 3, CH), f32), shape((CH, CH), f32))
    parts = call(parts_kernel, [], [depth, point, depth, point], 0, sums, done)
    return (grad.reshape(inputs.shape), *parts)


def solution(mesh):
    count, samples = (mesh.shape["space"], mesh.shape["dp"])
    ring = min(8, count // 2)
    grid = mesh.devices.reshape(count // (2 * ring), ring, 2, samples)
    split = jax.sharding.Mesh(grid, (*SPACE, "dp"))
    slabs = P("dp", SPACE, None, None, None, None)
    return jax.shard_map(
        on_device,
        mesh=split,
        in_specs=(slabs, P(), P(), P(), P(), slabs),
        out_specs=(slabs, P(), P(), P(), P()),
        check_vma=False,
    )
```

```python
import functools
import math

import jax
import jax.numpy as jnp
from jax import lax
from jax.experimental import pallas as pl
from jax.experimental.pallas import tpu as pltpu
from jax.sharding import PartitionSpec as P

CH = 128
LINE = 64
CELLS = 1024
PADDED = CELLS + 2 * LINE
ROWS = 256
TERMS = 320
VMEM_LIMIT = 24 * 1024 * 1024


def mm(a, b):
    return jnp.dot(a, b, preferred_element_type=jnp.float32)


def keep_mask(count, edge):
    return lax.broadcasted_iota(jnp.int32, (count, 1), 0) % LINE != edge


def from_before(v):
    return jnp.where(keep_mask(v.shape[0], 0), pltpu.roll(v, 1, 0), 0.0)


def from_after(v):
    return jnp.where(keep_mask(v.shape[0], LINE - 1), pltpu.roll(v, v.shape[0] - 1, 0), 0.0)


def shift_sum(products, width):
    return (
        from_before(products[:, :width])
        + products[:, width : 2 * width]
        + from_after(products[:, 2 * width :])
    )


def set_plane(ref, slot, plane):
    edge = jnp.zeros((LINE, CH), jnp.bfloat16)
    ref[slot, 0:LINE, :] = edge
    ref[slot, LINE : LINE + CELLS, :] = plane
    ref[slot, LINE + CELLS : PADDED, :] = edge


def local_products(planes, weights, start):
    left = jnp.concatenate(
        [
            planes[1 + p, start + b * LINE : start + b * LINE + ROWS, :]
            for p in range(2)
            for b in range(3)
        ],
        axis=1,
    )
    return shift_sum(mm(left, weights[...]), 2 * CH)


def side_products(planes, slots, weights, start):
    pairs = ROWS // LINE
    left = jnp.concatenate(
        [
            jnp.concatenate(
                [
                    planes[slot, start + (2 * j + i) * LINE : start + (2 * j + i + 1) * LINE, :]
                    for j in range(pairs)
                ],
                axis=0,
            )
            for slot in slots
            for i in range(4)
        ],
        axis=1,
    )
    out = shift_sum(mm(left, weights[...]), 2 * CH)
    return jnp.concatenate(
        [
            out[j * LINE : (j + 1) * LINE, q * CH : (q + 1) * CH]
            for j in range(pairs)
            for q in range(2)
        ],
        axis=0,
    )


def fill_local(ref, tap_matrix):
    for a in range(3):
        for b in range(3):
            for e in range(3):
                block = tap_matrix(9 * a + 3 * b + e)
                for p in range(2):
                    x = p + 1 - a
                    if 0 <= x < 2:
                        row, col = ((3 * p + b) * CH, (2 * e + x) * CH)
                        ref[row : row + CH, col : col + CH] = block


def fill_side(ref, tap_matrix, high):
    ref[...] = jnp.zeros(ref.shape, jnp.bfloat16)
    for b in range(3):
        for e in range(3):
            block = jnp.where(high, tap_matrix(18 + 3 * b + e), tap_matrix(3 * b + e))
            for q in range(2):
                row, col = ((b + q) * CH, (2 * e + q) * CH)
                ref[row : row + CH, col : col + CH] = block


def fill_lines(ref, tap_matrix):
    ref[...] = jnp.zeros(ref.shape, jnp.bfloat16)
    for a in range(3):
        for b in range(3):
            for e in range(3):
                block = tap_matrix(9 * a + 3 * b + e)
                for q in range(2):
                    row, col = ((4 * a + b + q) * CH, (2 * e + q) * CH)
                    ref[row : row + CH, col : col + CH] = block


def columns_of(depth):
    padded = jnp.concatenate([depth, jnp.zeros((CH - 27, CH), jnp.float32)], axis=0)
    return padded.T


def forward_taps(cols, point):
    return lambda s: (cols[:, s : s + 1] * point).astype(jnp.bfloat16)


def backward_taps(depth, point_t):
    return lambda s: (depth[26 - s : 27 - s, :] * point_t).astype(jnp.bfloat16)


def tap_sums(left_t, planes, x, combine):
    order = [(a, b) for a in range(3) for b in range(3)]
    for at in range(0, 9, 2):
        group = order[at : at + 2]
        right = jnp.concatenate(
            [planes[x + a, b * LINE : b * LINE + CELLS, :] for a, b in group], axis=1
        )
        sums = mm(left_t[...], right)
        for i, (a, b) in enumerate(group):
            for e in range(3):
                combine(9 * a + 3 * b + e, sums[e * CH : (e + 1) * CH, i * CH : (i + 1) * CH])


def activate(value, back, scaled_out, scaled_t, hidden_t, start):
    sigma = jax.nn.sigmoid(value)
    hidden = (value * sigma).astype(jnp.bfloat16).astype(jnp.float32)
    scaled = (back * (sigma * (1.0 + value * (1.0 - sigma)))).astype(jnp.bfloat16)
    scaled_out[start : start + ROWS, :] = scaled
    scaled = scaled.astype(jnp.float32)
    for ref, v in ((scaled_t, scaled), (hidden_t, hidden)):
        shifted = jnp.concatenate([from_after(v), v, from_before(v)], axis=1)
        ref[:, start : start + ROWS] = shifted.astype(jnp.bfloat16).T


def weight_terms(factor, x, planes_in, planes_up, scaled_t, hidden_t, weights, total, before, terms):
    depth_one, point_one, depth_two, point_two = weights
    point_one_t = point_one.T
    cols_two = columns_of(depth_two)
    lane = lax.broadcasted_iota(jnp.int32, (CH, CH), 1)
    total[...] = jnp.zeros((3, CH, CH), jnp.float32)
    terms[...] = jnp.zeros((TERMS, CH), jnp.float32) if before is None else before[...]

    def layer_one(s, block):
        total[0] += depth_one[s : s + 1, :] * block
        terms[s : s + 1, :] += jnp.sum(point_one_t * block, axis=0, keepdims=True) * factor

    tap_sums(scaled_t, planes_in, x, layer_one)
    terms[32:160, :] += total[0].T * factor

    def layer_two(s, block):
        s = 26 - s
        total[1] += cols_two[:, s : s + 1] * block
        total[2] += jnp.where(lane == s, jnp.sum(point_two * block, axis=1, keepdims=True), 0.0)

    tap_sums(hidden_t, planes_up, x, layer_two)
    terms[192:320, :] += total[1] * factor
    terms[160:192, :] += total[2].T[:32, :] * factor


def place_planes(planes, block, core, near, far):
    for x in range(2):
        set_plane(planes, 1 + x, block[x])
    if near is not None:
        set_plane(planes, 3 - 3 * core, near)
    if far is not None:
        set_plane(planes, 3 * core, far)


def near_kernel(
    factor,
    parity, block_in, block_up, near, d1, p1, d2, p2,
    scaled_out, pre, carried, far_w1, far_w2, terms,
    planes_in, planes_up, local_one, local_two, side_one, side_two, scaled_t, hidden_t, total,
):
    core = parity[0]
    inner = 1 - core
    weights = tuple(w[...].astype(jnp.float32) for w in (d1, p1, d2, p2))
    depth_one, point_one, depth_two, point_two = weights
    place_planes(planes_in, block_in, core, near[0], None)
    place_planes(planes_up, block_up, core, near[1], None)
    near_high = core == 0
    taps_one = forward_taps(columns_of(depth_one), point_one)
    taps_two = backward_taps(depth_two, point_two.T)
    for taps, local, side, other in (
        (taps_one, local_one, side_one, far_w1),
        (taps_two, local_two, side_two, far_w2),
    ):
        fill_local(local, taps)
        fill_side(side, taps, near_high)
        fill_side(other, taps, jnp.logical_not(near_high))
    near_slot = 3 - 3 * core
    for half in range(0, CELLS, 2 * ROWS):
        side_in = side_products(planes_in, (near_slot,), side_one, half)
        side_up = side_products(planes_up, (near_slot,), side_two, half)
        for at in range(0, 2 * ROWS, ROWS):
            start = half + at
            both_in = local_products(planes_in, local_one, start)
            both_up = local_products(planes_up, local_two, start)
            low, high = (both_in[:, :CH], both_in[:, CH:])
            pre[start : start + ROWS, :] = jnp.where(near_high, low, high)
            value = jnp.where(near_high, high, low) + side_in[at : at + ROWS, :]
            low, high = (both_up[:, :CH], both_up[:, CH:])
            carried[start : start + ROWS, :] = jnp.where(near_high, low, high)
            back = jnp.where(near_high, high, low) + side_up[at : at + ROWS, :]
            activate(value, back, scaled_out, scaled_t, hidden_t, start)
    weight_terms(
        factor, inner, planes_in, planes_up, scaled_t, hidden_t, weights, total, None, terms
    )


def far_kernel(
    factor,
    parity, block_in, block_up, far, pre, carried, far_w1, far_w2, d1, p1, d2, p2, before,
    scaled_out, terms,
    planes_in, planes_up, scaled_t, hidden_t, total,
):
    core = parity[0]
    weights = tuple(w[...].astype(jnp.float32) for w in (d1, p1, d2, p2))
    place_planes(planes_in, block_in, core, None, far[0])
    place_planes(planes_up, block_up, core, None, far[1])
    for half in range(0, CELLS, 2 * ROWS):
        side_in = side_products(planes_in, (3 * core,), far_w1, half)
        side_up = side_products(planes_up, (3 * core,), far_w2, half)
        for at in range(0, 2 * ROWS, ROWS):
            start = half + at
            value = side_in[at : at + ROWS, :] + pre[start : start + ROWS, :]
            back = side_up[at : at + ROWS, :] + carried[start : start + ROWS, :]
            activate(value, back, scaled_out, scaled_t, hidden_t, start)
    weight_terms(
        factor, core, planes_in, planes_up, scaled_t, hidden_t, weights, total, before, terms
    )


def beside_kernel(
    place, block_in, block_up, far, beyond, d1, p1, d2, p2,
    scaled_out,
    planes_in, planes_up, w_one, w_two,
):
    core = place[0]
    depth_one, point_one, depth_two, point_two = (
        w[...].astype(jnp.float32) for w in (d1, p1, d2, p2)
    )
    for which, planes, block in ((0, planes_in, block_in), (1, planes_up, block_up)):
        set_plane(planes, 2 * core, beyond[which])
        set_plane(planes, 1, far[which])
        set_plane(planes, 2 - 2 * core, block[core])
    fill_lines(w_one, forward_taps(columns_of(depth_one), point_one))
    fill_lines(w_two, backward_taps(depth_two, point_two.T))
    inside = place[1] > 0
    for half in range(0, CELLS, 2 * ROWS):
        value = side_products(planes_in, (0, 1, 2), w_one, half)
        back = side_products(planes_up, (0, 1, 2), w_two, half)
        sigma = jax.nn.sigmoid(value)
        scaled = back * (sigma * (1.0 + value * (1.0 - sigma)))
        scaled_out[half : half + 2 * ROWS, :] = jnp.where(inside, scaled, 0.0).astype(jnp.bfloat16)


def last_kernel(parity, inner, outer, near, far, d1, p1, out, done, planes, local, low_side, high_side):
    core = parity[0]
    depth_one = d1[...].astype(jnp.float32)
    taps = backward_taps(depth_one, p1[...].astype(jnp.float32).T)
    fill_local(local, taps)
    fill_side(low_side, taps, False)
    fill_side(high_side, taps, True)
    set_plane(planes, 2 - core, inner[...])
    set_plane(planes, 1 + core, outer[...])
    set_plane(planes, 3 - 3 * core, near[...])
    set_plane(planes, 3 * core, far[...])
    for half in range(0, CELLS, 2 * ROWS):
        low = side_products(planes, (0,), low_side, half)
        high = side_products(planes, (3,), high_side, half)
        for at in range(0, 2 * ROWS, ROWS):
            start = half + at
            both = local_products(planes, local, start)
            grad = both[:, :CH] + low[at : at + ROWS, :]
            out[0, start : start + ROWS, :] = grad.astype(jnp.bfloat16)
            grad = both[:, CH:] + high[at : at + ROWS, :]
            out[1, start : start + ROWS, :] = grad.astype(jnp.bfloat16)
    done[...] = jnp.zeros((8, CH), jnp.float32)


def parts_kernel(sums, done, depth_one, point_one, depth_two, point_two):
    for a in range(3):
        for b in range(3):
            row = 9 * a + 3 * b
            depth_one[a, b] = sums[row : row + 3, :]
            depth_two[a, b] = sums[160 + row : 163 + row, :]
    point_one[...] = sums[32:160, :]
    point_two[...] = sums[192:320, :]


def call(kernel, scratch, outs, flops, *args):
    vmem = pl.BlockSpec(memory_space=pltpu.VMEM)
    smem = pl.BlockSpec(memory_space=pltpu.SMEM)
    moved = sum(a.size * a.dtype.itemsize for a in args) + sum(
        o.size * o.dtype.itemsize for o in outs
    )
    return pl.pallas_call(
        kernel,
        out_shape=outs,
        in_specs=[smem if a.dtype == jnp.int32 else vmem for a in args],
        out_specs=[vmem] * len(outs),
        scratch_shapes=scratch,
        cost_estimate=pl.CostEstimate(flops=flops, bytes_accessed=moved, transcendentals=0),
        compiler_params=pltpu.CompilerParams(vmem_limit_bytes=VMEM_LIMIT),
    )(*args)


SPACE = ("outer", "ring", "core")
ACROSS = ("outer", "core", "dp")


def with_other_core(v):
    return lax.ppermute(v, "core", [(0, 1), (1, 0)])


def with_other_chip(v):
    count = math.prod(lax.axis_size(name) for name in SPACE)
    pairs = [(i, i + 1) for i in range(1, count - 1, 2)]
    return lax.ppermute(v, SPACE, pairs + [(j, i) for i, j in pairs])


def sent_across(terms):
    count = math.prod(lax.axis_size(name) for name in ACROSS)
    tiles = terms.reshape(count, 1, -1)
    return lax.all_to_all(tiles, ACROSS, 0, 0, tiled=True)


def reduced_around(share):
    copies = jnp.broadcast_to(share, (lax.axis_size("ring"), *share.shape))
    return lax.all_to_all(copies, "ring", 0, 0, tiled=True).sum(axis=0)


def gathered_across(share):
    count = math.prod(lax.axis_size(name) for name in ACROSS)
    copies = jnp.broadcast_to(share, (count, *share.shape))
    return lax.all_to_all(copies, ACROSS, 0, 0, tiled=True).reshape(TERMS, CH)


def on_device(inputs, depth_one, point_one, depth_two, point_two, cotangent):
    f32, bf16 = jnp.float32, jnp.bfloat16
    shape = jax.ShapeDtypeStruct
    block_in = inputs.reshape(2, CELLS, CH)
    block_up = cotangent.reshape(2, CELLS, CH)
    d1 = depth_one.reshape(27, CH)
    d2 = depth_two.reshape(27, CH)
    core = lax.axis_index("core")
    count = math.prod(lax.axis_size(name) for name in SPACE)
    index = lax.axis_index(SPACE)
    inside = jnp.logical_and(index > 0, index < count - 1)
    place = jnp.stack([core, inside]).astype(jnp.int32)


    def both(x):
        return jnp.concatenate(
            [lax.dynamic_slice_in_dim(block, x, 1, 0) for block in (block_in, block_up)], axis=0
        )

    beside = both(1 - core)
    far = with_other_chip(both(core))
    near = with_other_core(beside)
    slots = pltpu.VMEM((4, PADDED, CH), bf16)
    local_w = pltpu.VMEM((6 * CH, 6 * CH), bf16)
    side_w = pltpu.VMEM((4 * CH, 6 * CH), bf16)
    flipped = pltpu.VMEM((3 * CH, CELLS), bf16)
    totals = pltpu.VMEM((3, CH, CH), f32)
    devices = math.prod(lax.axis_size(name) for name in ("dp", *SPACE))
    factor = 1.0 / math.sqrt(devices * 2 * CELLS)
    inner, pre, carried, far_w1, far_w2, terms = call(
        functools.partial(near_kernel, factor),
        [slots, slots, local_w, local_w, side_w, side_w, flipped, flipped, totals],
        [shape((CELLS, CH), bf16)]
        + [shape((CELLS, CH), f32)] * 2
        + [shape((4 * CH, 6 * CH), bf16)] * 2
        + [shape((TERMS, CH), f32)],
        8_000_000_000,
        place, block_in, block_up, near, d1, point_one, d2, point_two,
    )
    beside, inner = lax.optimization_barrier((beside, inner))
    beyond = with_other_chip(beside)
    inner_beside = with_other_core(inner)
    outer, terms = call(
        functools.partial(far_kernel, factor),
        [slots, slots, flipped, flipped, totals],
        [shape((CELLS, CH), bf16), shape((TERMS, CH), f32)],
        4_000_000_000,
        place, block_in, block_up, far, pre, carried, far_w1, far_w2,
        d1, point_one, d2, point_two, terms,
    )
    share = sent_across(terms).sum(axis=0)
    lines_w = pltpu.VMEM((12 * CH, 6 * CH), bf16)
    (outer_beside,) = call(
        beside_kernel,
        [slots, slots, lines_w, lines_w],
        [shape((CELLS, CH), bf16)],
        6_000_000_000,
        place, block_in, block_up, far, beyond, d1, point_one, d2, point_two,
    )
    grad, done = call(
        last_kernel,
        [slots, local_w, side_w, side_w],
        [shape((2, CELLS, CH), bf16), shape((8, CH), f32)],
        4_000_000_000,
        place, inner, outer, inner_beside, outer_beside, d1, point_one,
    )
    sums = gathered_across(reduced_around(share))
    depth, point = (shape((3, 3, 3, CH), f32), shape((CH, CH), f32))
    parts = call(parts_kernel, [], [depth, point, depth, point], 0, sums, done)
    return (grad.reshape(inputs.shape), *parts)


def solution(mesh):
    count, samples = (mesh.shape["space"], mesh.shape["dp"])
    ring = min(8, count // 2)
    grid = mesh.devices.reshape(count // (2 * ring), ring, 2, samples)
    split = jax.sharding.Mesh(grid, (*SPACE, "dp"))
    slabs = P("dp", SPACE, None, None, None, None)
    return jax.shard_map(
        on_device,
        mesh=split,
        in_specs=(slabs, P(), P(), P(), P(), slabs),
        out_specs=(slabs, P(), P(), P(), P()),
        check_vma=False,
    )
```

```python
import functools
import math

import jax
import jax.numpy as jnp
from jax import lax
from jax.experimental import pallas as pl
from jax.experimental.pallas import tpu as pltpu
from jax.sharding import PartitionSpec as P

CH = 128
LINE = 64
CELLS = 1024
PADDED = CELLS + 2 * LINE
ROWS = 256
TERMS = 320
VMEM_LIMIT = 24 * 1024 * 1024


def mm(a, b):
    return jnp.dot(a, b, preferred_element_type=jnp.float32)


def keep_mask(count, edge):
    return lax.broadcasted_iota(jnp.int32, (count, 1), 0) % LINE != edge


def from_before(v):
    return jnp.where(keep_mask(v.shape[0], 0), pltpu.roll(v, 1, 0), 0.0)


def from_after(v):
    return jnp.where(keep_mask(v.shape[0], LINE - 1), pltpu.roll(v, v.shape[0] - 1, 0), 0.0)


def shift_sum(products, width):
    return (
        from_before(products[:, :width])
        + products[:, width : 2 * width]
        + from_after(products[:, 2 * width :])
    )


def set_plane(ref, slot, plane):
    edge = jnp.zeros((LINE, CH), jnp.bfloat16)
    ref[slot, 0:LINE, :] = edge
    ref[slot, LINE : LINE + CELLS, :] = plane
    ref[slot, LINE + CELLS : PADDED, :] = edge


def local_products(planes, weights, start):
    left = jnp.concatenate(
        [
            planes[1 + p, start + b * LINE : start + b * LINE + ROWS, :]
            for p in range(2)
            for b in range(3)
        ],
        axis=1,
    )
    return shift_sum(mm(left, weights[...]), 2 * CH)


def side_products(planes, slot, weights, start):
    pairs = ROWS // LINE
    left = jnp.concatenate(
        [
            jnp.concatenate(
                [
                    planes[slot, start + (2 * j + i) * LINE : start + (2 * j + i + 1) * LINE, :]
                    for j in range(pairs)
                ],
                axis=0,
            )
            for i in range(4)
        ],
        axis=1,
    )
    out = shift_sum(mm(left, weights[...]), 2 * CH)
    return jnp.concatenate(
        [
            out[j * LINE : (j + 1) * LINE, q * CH : (q + 1) * CH]
            for j in range(pairs)
            for q in range(2)
        ],
        axis=0,
    )


def fill_local(ref, tap_matrix):
    for a in range(3):
        for b in range(3):
            for e in range(3):
                block = tap_matrix(9 * a + 3 * b + e)
                for p in range(2):
                    x = p + 1 - a
                    if 0 <= x < 2:
                        row, col = ((3 * p + b) * CH, (2 * e + x) * CH)
                        ref[row : row + CH, col : col + CH] = block


def fill_side(ref, tap_matrix, high):
    ref[...] = jnp.zeros(ref.shape, jnp.bfloat16)
    for b in range(3):
        for e in range(3):
            block = jnp.where(high, tap_matrix(18 + 3 * b + e), tap_matrix(3 * b + e))
            for q in range(2):
                row, col = ((b + q) * CH, (2 * e + q) * CH)
                ref[row : row + CH, col : col + CH] = block


def columns_of(depth):
    padded = jnp.concatenate([depth, jnp.zeros((CH - 27, CH), jnp.float32)], axis=0)
    return padded.T


def forward_taps(cols, point):
    return lambda s: (cols[:, s : s + 1] * point).astype(jnp.bfloat16)


def backward_taps(depth, point_t):
    return lambda s: (depth[26 - s : 27 - s, :] * point_t).astype(jnp.bfloat16)


def tap_sums(left_t, planes, x, combine):
    order = [(a, b) for a in range(3) for b in range(3)]
    for at in range(0, 9, 2):
        group = order[at : at + 2]
        right = jnp.concatenate(
            [planes[x + a, b * LINE : b * LINE + CELLS, :] for a, b in group], axis=1
        )
        sums = mm(left_t[...], right)
        for i, (a, b) in enumerate(group):
            for e in range(3):
                combine(9 * a + 3 * b + e, sums[e * CH : (e + 1) * CH, i * CH : (i + 1) * CH])


def activate(value, back, scaled_out, scaled_t, hidden_t, start):
    sigma = jax.nn.sigmoid(value)
    hidden = (value * sigma).astype(jnp.bfloat16).astype(jnp.float32)
    scaled = (back * (sigma * (1.0 + value * (1.0 - sigma)))).astype(jnp.bfloat16)
    scaled_out[start : start + ROWS, :] = scaled
    scaled = scaled.astype(jnp.float32)
    for ref, v in ((scaled_t, scaled), (hidden_t, hidden)):
        shifted = jnp.concatenate([from_after(v), v, from_before(v)], axis=1)
        ref[:, start : start + ROWS] = shifted.astype(jnp.bfloat16).T


def weight_terms(factor, x, planes_in, planes_up, scaled_t, hidden_t, weights, total, before, terms):
    depth_one, point_one, depth_two, point_two = weights
    point_one_t = point_one.T
    cols_two = columns_of(depth_two)
    lane = lax.broadcasted_iota(jnp.int32, (CH, CH), 1)
    total[...] = jnp.zeros((3, CH, CH), jnp.float32)
    terms[...] = jnp.zeros((TERMS, CH), jnp.float32) if before is None else before[...]

    def layer_one(s, block):
        total[0] += depth_one[s : s + 1, :] * block
        terms[s : s + 1, :] += jnp.sum(point_one_t * block, axis=0, keepdims=True) * factor

    tap_sums(scaled_t, planes_in, x, layer_one)
    terms[32:160, :] += total[0].T * factor

    def layer_two(s, block):
        s = 26 - s
        total[1] += cols_two[:, s : s + 1] * block
        total[2] += jnp.where(lane == s, jnp.sum(point_two * block, axis=1, keepdims=True), 0.0)

    tap_sums(hidden_t, planes_up, x, layer_two)
    terms[192:320, :] += total[1] * factor
    terms[160:192, :] += total[2].T[:32, :] * factor


def place_planes(planes, block, core, near, far):
    for x in range(2):
        set_plane(planes, 1 + x, block[x])
    if near is not None:
        set_plane(planes, 3 - 3 * core, near)
    if far is not None:
        set_plane(planes, 3 * core, far)


def taps_kernel(
    parity, d1, p1, d2, p2, local_one, local_two, side_one, side_two, far_w1, far_w2
):
    near_high = parity[0] == 0
    depth_one, point_one, depth_two, point_two = (
        w[...].astype(jnp.float32) for w in (d1, p1, d2, p2)
    )
    taps_one = forward_taps(columns_of(depth_one), point_one)
    taps_two = backward_taps(depth_two, point_two.T)
    for taps, local, side, other in (
        (taps_one, local_one, side_one, far_w1),
        (taps_two, local_two, side_two, far_w2),
    ):
        fill_local(local, taps)
        fill_side(side, taps, near_high)
        fill_side(other, taps, jnp.logical_not(near_high))


def near_kernel(
    factor,
    parity, block_in, block_up, near, local_one, local_two, side_one, side_two, d1, p1, d2, p2,
    scaled_out, pre, carried, terms,
    planes_in, planes_up, scaled_t, hidden_t, total,
):
    core = parity[0]
    inner = 1 - core
    weights = tuple(w[...].astype(jnp.float32) for w in (d1, p1, d2, p2))
    place_planes(planes_in, block_in, core, near[0], None)
    place_planes(planes_up, block_up, core, near[1], None)
    near_high = core == 0
    near_slot = 3 - 3 * core
    for half in range(0, CELLS, 2 * ROWS):
        side_in = side_products(planes_in, near_slot, side_one, half)
        side_up = side_products(planes_up, near_slot, side_two, half)
        for at in range(0, 2 * ROWS, ROWS):
            start = half + at
            both_in = local_products(planes_in, local_one, start)
            both_up = local_products(planes_up, local_two, start)
            low, high = (both_in[:, :CH], both_in[:, CH:])
            pre[start : start + ROWS, :] = jnp.where(near_high, low, high)
            value = jnp.where(near_high, high, low) + side_in[at : at + ROWS, :]
            low, high = (both_up[:, :CH], both_up[:, CH:])
            carried[start : start + ROWS, :] = jnp.where(near_high, low, high)
            back = jnp.where(near_high, high, low) + side_up[at : at + ROWS, :]
            activate(value, back, scaled_out, scaled_t, hidden_t, start)
    weight_terms(
        factor, inner, planes_in, planes_up, scaled_t, hidden_t, weights, total, None, terms
    )


def far_kernel(
    factor,
    parity, block_in, block_up, far, pre, carried, far_w1, far_w2, d1, p1, d2, p2, before,
    scaled_out, terms,
    planes_in, planes_up, scaled_t, hidden_t, total,
):
    core = parity[0]
    weights = tuple(w[...].astype(jnp.float32) for w in (d1, p1, d2, p2))
    place_planes(planes_in, block_in, core, None, far[0])
    place_planes(planes_up, block_up, core, None, far[1])
    for half in range(0, CELLS, 2 * ROWS):
        side_in = side_products(planes_in, 3 * core, far_w1, half)
        side_up = side_products(planes_up, 3 * core, far_w2, half)
        for at in range(0, 2 * ROWS, ROWS):
            start = half + at
            value = side_in[at : at + ROWS, :] + pre[start : start + ROWS, :]
            back = side_up[at : at + ROWS, :] + carried[start : start + ROWS, :]
            activate(value, back, scaled_out, scaled_t, hidden_t, start)
    weight_terms(
        factor, core, planes_in, planes_up, scaled_t, hidden_t, weights, total, before, terms
    )


def last_kernel(parity, inner, outer, near, far, d1, p1, out, done, planes, local, low_side, high_side):
    core = parity[0]
    depth_one = d1[...].astype(jnp.float32)
    taps = backward_taps(depth_one, p1[...].astype(jnp.float32).T)
    fill_local(local, taps)
    fill_side(low_side, taps, False)
    fill_side(high_side, taps, True)
    set_plane(planes, 2 - core, inner[...])
    set_plane(planes, 1 + core, outer[...])
    set_plane(planes, 3 - 3 * core, near[...])
    set_plane(planes, 3 * core, far[...])
    for half in range(0, CELLS, 2 * ROWS):
        low = side_products(planes, 0, low_side, half)
        high = side_products(planes, 3, high_side, half)
        for at in range(0, 2 * ROWS, ROWS):
            start = half + at
            both = local_products(planes, local, start)
            grad = both[:, :CH] + low[at : at + ROWS, :]
            out[0, start : start + ROWS, :] = grad.astype(jnp.bfloat16)
            grad = both[:, CH:] + high[at : at + ROWS, :]
            out[1, start : start + ROWS, :] = grad.astype(jnp.bfloat16)
    done[...] = jnp.zeros((8, CH), jnp.float32)


def sum_kernel(arrived, copies):
    total = arrived[0]
    for i in range(1, arrived.shape[0]):
        total = total + arrived[i]
    for i in range(copies.shape[0]):
        copies[i] = total


def parts_kernel(sums, done, depth_one, point_one, depth_two, point_two):
    for a in range(3):
        for b in range(3):
            row = 9 * a + 3 * b
            depth_one[a, b] = sums[row : row + 3, :]
            depth_two[a, b] = sums[160 + row : 163 + row, :]
    point_one[...] = sums[32:160, :]
    point_two[...] = sums[192:320, :]


def call(kernel, scratch, outs, flops, *args):
    vmem = pl.BlockSpec(memory_space=pltpu.VMEM)
    smem = pl.BlockSpec(memory_space=pltpu.SMEM)
    moved = sum(a.size * a.dtype.itemsize for a in args) + sum(
        o.size * o.dtype.itemsize for o in outs
    )
    return pl.pallas_call(
        kernel,
        out_shape=outs,
        in_specs=[smem if a.dtype == jnp.int32 else vmem for a in args],
        out_specs=[vmem] * len(outs),
        scratch_shapes=scratch,
        cost_estimate=pl.CostEstimate(flops=flops, bytes_accessed=moved, transcendentals=0),
        compiler_params=pltpu.CompilerParams(vmem_limit_bytes=VMEM_LIMIT),
    )(*args)


SPACE = ("outer", "ring", "core")
ACROSS = ("outer", "core", "dp")


def with_other_core(v):
    return lax.ppermute(v, "core", [(0, 1), (1, 0)])


def with_other_chip(v):
    count = math.prod(lax.axis_size(name) for name in SPACE)
    pairs = [(i, i + 1) for i in range(1, count - 1, 2)]
    return lax.ppermute(v, SPACE, pairs + [(j, i) for i, j in pairs])


def reduced_across(terms):
    count = math.prod(lax.axis_size(name) for name in ACROSS)
    tiles = terms.reshape(count, 1, -1)
    return lax.all_to_all(tiles, ACROSS, 0, 0, tiled=True).sum(axis=0)


def reduced_around(share):
    copies = jnp.broadcast_to(share, (lax.axis_size("ring"), *share.shape))
    arrived = lax.all_to_all(copies, "ring", 0, 0, tiled=True)
    count = math.prod(lax.axis_size(name) for name in ACROSS)
    (copies,) = call(
        sum_kernel, [], [jax.ShapeDtypeStruct((count, *share.shape), share.dtype)], 0, arrived
    )
    return copies


def gathered_across(copies):
    return lax.all_to_all(copies, ACROSS, 0, 0, tiled=True).reshape(TERMS, CH)


def on_device(inputs, depth_one, point_one, depth_two, point_two, cotangent):
    f32, bf16 = jnp.float32, jnp.bfloat16
    shape = jax.ShapeDtypeStruct
    block_in = inputs.reshape(2, CELLS, CH)
    block_up = cotangent.reshape(2, CELLS, CH)
    d1 = depth_one.reshape(27, CH)
    d2 = depth_two.reshape(27, CH)
    core = lax.axis_index("core")
    parity = core.astype(jnp.int32).reshape(1)


    def both(x):
        return jnp.concatenate(
            [lax.dynamic_slice_in_dim(block, x, 1, 0) for block in (block_in, block_up)], axis=0
        )

    outer = both(core)
    outer, inner = lax.optimization_barrier((outer, 1 - core))
    far = with_other_chip(outer)
    near = with_other_core(both(inner))
    slots = pltpu.VMEM((4, PADDED, CH), bf16)
    local_w = pltpu.VMEM((6 * CH, 6 * CH), bf16)
    side_w = pltpu.VMEM((4 * CH, 6 * CH), bf16)
    flipped = pltpu.VMEM((3 * CH, CELLS), bf16)
    totals = pltpu.VMEM((3, CH, CH), f32)
    devices = math.prod(lax.axis_size(name) for name in ("dp", *SPACE))
    factor = 1.0 / math.sqrt(devices * 2 * CELLS)
    local_one, local_two, side_one, side_two, far_w1, far_w2 = call(
        taps_kernel,
        [],
        [shape((6 * CH, 6 * CH), bf16)] * 2 + [shape((4 * CH, 6 * CH), bf16)] * 4,
        1_000_000_000,
        parity, d1, point_one, d2, point_two,
    )
    inner, pre, carried, terms = call(
        functools.partial(near_kernel, factor),
        [slots, slots, flipped, flipped, totals],
        [shape((CELLS, CH), bf16)] + [shape((CELLS, CH), f32)] * 2 + [shape((TERMS, CH), f32)],
        6_000_000_000,
        parity, block_in, block_up, near, local_one, local_two, side_one, side_two,
        d1, point_one, d2, point_two,
    )
    outer, terms = call(
        functools.partial(far_kernel, factor),
        [slots, slots, flipped, flipped, totals],
        [shape((CELLS, CH), bf16), shape((TERMS, CH), f32)],
        4_000_000_000,
        parity, block_in, block_up, far, pre, carried, far_w1, far_w2,
        d1, point_one, d2, point_two, terms,
    )
    share = reduced_across(terms)
    outer_beside = with_other_chip(outer)
    inner_beside = with_other_core(inner)
    grad, done = call(
        last_kernel,
        [slots, local_w, side_w, side_w],
        [shape((2, CELLS, CH), bf16), shape((8, CH), f32)],
        4_000_000_000,
        parity, inner, outer, inner_beside, outer_beside, d1, point_one,
    )
    sums = gathered_across(reduced_around(share))
    depth, point = (shape((3, 3, 3, CH), f32), shape((CH, CH), f32))
    parts = call(parts_kernel, [], [depth, point, depth, point], 0, sums, done)
    return (grad.reshape(inputs.shape), *parts)


def solution(mesh):
    count, samples = (mesh.shape["space"], mesh.shape["dp"])
    ring = min(8, count // 2)
    grid = mesh.devices.reshape(count // (2 * ring), ring, 2, samples)
    split = jax.sharding.Mesh(grid, (*SPACE, "dp"))
    slabs = P("dp", SPACE, None, None, None, None)
    return jax.shard_map(
        on_device,
        mesh=split,
        in_specs=(slabs, P(), P(), P(), P(), slabs),
        out_specs=(slabs, P(), P(), P(), P()),
        check_vma=False,
    )
```

```python
import functools
import math

import jax
import jax.numpy as jnp
from jax import lax
from jax.experimental import pallas as pl
from jax.experimental.pallas import tpu as pltpu
from jax.sharding import PartitionSpec as P

CH = 128
LINE = 64
CELLS = 1024
PADDED = CELLS + 2 * LINE
ROWS = 256
TERMS = 320
VMEM_LIMIT = 24 * 1024 * 1024


def mm(a, b):
    return jnp.dot(a, b, preferred_element_type=jnp.float32)


def keep_mask(count, edge):
    return lax.broadcasted_iota(jnp.int32, (count, 1), 0) % LINE != edge


def from_before(v):
    return jnp.where(keep_mask(v.shape[0], 0), pltpu.roll(v, 1, 0), 0.0)


def from_after(v):
    return jnp.where(keep_mask(v.shape[0], LINE - 1), pltpu.roll(v, v.shape[0] - 1, 0), 0.0)


def shift_sum(products, width):
    return (
        from_before(products[:, :width])
        + products[:, width : 2 * width]
        + from_after(products[:, 2 * width :])
    )


def set_plane(ref, slot, plane):
    edge = jnp.zeros((LINE, CH), jnp.bfloat16)
    ref[slot, 0:LINE, :] = edge
    ref[slot, LINE : LINE + CELLS, :] = plane
    ref[slot, LINE + CELLS : PADDED, :] = edge


def local_products(planes, weights, start):
    left = jnp.concatenate(
        [
            planes[1 + p, start + b * LINE : start + b * LINE + ROWS, :]
            for p in range(2)
            for b in range(3)
        ],
        axis=1,
    )
    return shift_sum(mm(left, weights[...]), 2 * CH)


def side_products(planes, slot, weights, start):
    pairs = ROWS // LINE
    left = jnp.concatenate(
        [
            jnp.concatenate(
                [
                    planes[slot, start + (2 * j + i) * LINE : start + (2 * j + i + 1) * LINE, :]
                    for j in range(pairs)
                ],
                axis=0,
            )
            for i in range(4)
        ],
        axis=1,
    )
    out = shift_sum(mm(left, weights[...]), 2 * CH)
    return jnp.concatenate(
        [
            out[j * LINE : (j + 1) * LINE, q * CH : (q + 1) * CH]
            for j in range(pairs)
            for q in range(2)
        ],
        axis=0,
    )


def fill_local(ref, tap_matrix):
    for a in range(3):
        for b in range(3):
            for e in range(3):
                block = tap_matrix(9 * a + 3 * b + e)
                for p in range(2):
                    x = p + 1 - a
                    if 0 <= x < 2:
                        row, col = ((3 * p + b) * CH, (2 * e + x) * CH)
                        ref[row : row + CH, col : col + CH] = block


def fill_side(ref, tap_matrix, high):
    ref[...] = jnp.zeros(ref.shape, jnp.bfloat16)
    for b in range(3):
        for e in range(3):
            block = jnp.where(high, tap_matrix(18 + 3 * b + e), tap_matrix(3 * b + e))
            for q in range(2):
                row, col = ((b + q) * CH, (2 * e + q) * CH)
                ref[row : row + CH, col : col + CH] = block


def columns_of(depth):
    padded = jnp.concatenate([depth, jnp.zeros((CH - 27, CH), jnp.float32)], axis=0)
    return padded.T


def forward_taps(cols, point):
    return lambda s: (cols[:, s : s + 1] * point).astype(jnp.bfloat16)


def backward_taps(depth, point_t):
    return lambda s: (depth[26 - s : 27 - s, :] * point_t).astype(jnp.bfloat16)


def tap_sums(left_t, planes, x, combine):
    order = [(a, b) for a in range(3) for b in range(3)]
    for at in range(0, 9, 2):
        group = order[at : at + 2]
        right = jnp.concatenate(
            [planes[x + a, b * LINE : b * LINE + CELLS, :] for a, b in group], axis=1
        )
        sums = mm(left_t[...], right)
        for i, (a, b) in enumerate(group):
            for e in range(3):
                combine(9 * a + 3 * b + e, sums[e * CH : (e + 1) * CH, i * CH : (i + 1) * CH])


def activate(value, back, scaled_out, scaled_t, hidden_t, start):
    sigma = jax.nn.sigmoid(value)
    hidden = (value * sigma).astype(jnp.bfloat16).astype(jnp.float32)
    scaled = (back * (sigma * (1.0 + value * (1.0 - sigma)))).astype(jnp.bfloat16)
    scaled_out[start : start + ROWS, :] = scaled
    scaled = scaled.astype(jnp.float32)
    for ref, v in ((scaled_t, scaled), (hidden_t, hidden)):
        shifted = jnp.concatenate([from_after(v), v, from_before(v)], axis=1)
        ref[:, start : start + ROWS] = shifted.astype(jnp.bfloat16).T


def weight_terms(factor, x, planes_in, planes_up, scaled_t, hidden_t, weights, total, before, terms):
    depth_one, point_one, depth_two, point_two = weights
    point_one_t = point_one.T
    cols_two = columns_of(depth_two)
    lane = lax.broadcasted_iota(jnp.int32, (CH, CH), 1)
    total[...] = jnp.zeros((3, CH, CH), jnp.float32)
    terms[...] = jnp.zeros((TERMS, CH), jnp.float32) if before is None else before[...]

    def layer_one(s, block):
        total[0] += depth_one[s : s + 1, :] * block
        terms[s : s + 1, :] += jnp.sum(point_one_t * block, axis=0, keepdims=True) * factor

    tap_sums(scaled_t, planes_in, x, layer_one)
    terms[32:160, :] += total[0].T * factor

    def layer_two(s, block):
        s = 26 - s
        total[1] += cols_two[:, s : s + 1] * block
        total[2] += jnp.where(lane == s, jnp.sum(point_two * block, axis=1, keepdims=True), 0.0)

    tap_sums(hidden_t, planes_up, x, layer_two)
    terms[192:320, :] += total[1] * factor
    terms[160:192, :] += total[2].T[:32, :] * factor


def place_planes(planes, block, core, near, far):
    for x in range(2):
        set_plane(planes, 1 + x, block[x])
    if near is not None:
        set_plane(planes, 3 - 3 * core, near)
    if far is not None:
        set_plane(planes, 3 * core, far)


def taps_kernel(
    parity, d1, p1, d2, p2, local_one, local_two, side_one, side_two, far_w1, far_w2
):
    near_high = parity[0] == 0
    depth_one, point_one, depth_two, point_two = (
        w[...].astype(jnp.float32) for w in (d1, p1, d2, p2)
    )
    taps_one = forward_taps(columns_of(depth_one), point_one)
    taps_two = backward_taps(depth_two, point_two.T)
    for taps, local, side, other in (
        (taps_one, local_one, side_one, far_w1),
        (taps_two, local_two, side_two, far_w2),
    ):
        fill_local(local, taps)
        fill_side(side, taps, near_high)
        fill_side(other, taps, jnp.logical_not(near_high))


def near_kernel(
    factor,
    parity, block_in, block_up, near, local_one, local_two, side_one, side_two, d1, p1, d2, p2,
    scaled_out, pre, carried, terms,
    planes_in, planes_up, scaled_t, hidden_t, total,
):
    core = parity[0]
    inner = 1 - core
    weights = tuple(w[...].astype(jnp.float32) for w in (d1, p1, d2, p2))
    place_planes(planes_in, block_in, core, near[0], None)
    place_planes(planes_up, block_up, core, near[1], None)
    near_high = core == 0
    near_slot = 3 - 3 * core
    for half in range(0, CELLS, 2 * ROWS):
        side_in = side_products(planes_in, near_slot, side_one, half)
        side_up = side_products(planes_up, near_slot, side_two, half)
        for at in range(0, 2 * ROWS, ROWS):
            start = half + at
            both_in = local_products(planes_in, local_one, start)
            both_up = local_products(planes_up, local_two, start)
            low, high = (both_in[:, :CH], both_in[:, CH:])
            pre[start : start + ROWS, :] = jnp.where(near_high, low, high)
            value = jnp.where(near_high, high, low) + side_in[at : at + ROWS, :]
            low, high = (both_up[:, :CH], both_up[:, CH:])
            carried[start : start + ROWS, :] = jnp.where(near_high, low, high)
            back = jnp.where(near_high, high, low) + side_up[at : at + ROWS, :]
            activate(value, back, scaled_out, scaled_t, hidden_t, start)
    weight_terms(
        factor, inner, planes_in, planes_up, scaled_t, hidden_t, weights, total, None, terms
    )


def far_kernel(
    factor,
    parity, block_in, block_up, far, pre, carried, far_w1, far_w2, d1, p1, d2, p2, before,
    scaled_out, terms,
    planes_in, planes_up, scaled_t, hidden_t, total,
):
    core = parity[0]
    weights = tuple(w[...].astype(jnp.float32) for w in (d1, p1, d2, p2))
    place_planes(planes_in, block_in, core, None, far[0])
    place_planes(planes_up, block_up, core, None, far[1])
    for half in range(0, CELLS, 2 * ROWS):
        side_in = side_products(planes_in, 3 * core, far_w1, half)
        side_up = side_products(planes_up, 3 * core, far_w2, half)
        for at in range(0, 2 * ROWS, ROWS):
            start = half + at
            value = side_in[at : at + ROWS, :] + pre[start : start + ROWS, :]
            back = side_up[at : at + ROWS, :] + carried[start : start + ROWS, :]
            activate(value, back, scaled_out, scaled_t, hidden_t, start)
    weight_terms(
        factor, core, planes_in, planes_up, scaled_t, hidden_t, weights, total, before, terms
    )


def last_kernel(parity, inner, outer, near, far, d1, p1, out, done, planes, local, low_side, high_side):
    core = parity[0]
    depth_one = d1[...].astype(jnp.float32)
    taps = backward_taps(depth_one, p1[...].astype(jnp.float32).T)
    fill_local(local, taps)
    fill_side(low_side, taps, False)
    fill_side(high_side, taps, True)
    set_plane(planes, 2 - core, inner[...])
    set_plane(planes, 1 + core, outer[...])
    set_plane(planes, 3 - 3 * core, near[...])
    set_plane(planes, 3 * core, far[...])
    for half in range(0, CELLS, 2 * ROWS):
        low = side_products(planes, 0, low_side, half)
        high = side_products(planes, 3, high_side, half)
        for at in range(0, 2 * ROWS, ROWS):
            start = half + at
            both = local_products(planes, local, start)
            grad = both[:, :CH] + low[at : at + ROWS, :]
            out[0, start : start + ROWS, :] = grad.astype(jnp.bfloat16)
            grad = both[:, CH:] + high[at : at + ROWS, :]
            out[1, start : start + ROWS, :] = grad.astype(jnp.bfloat16)
    done[...] = jnp.zeros((8, CH), jnp.float32)


def sum_kernel(arrived, copies):
    total = arrived[0]
    for i in range(1, arrived.shape[0]):
        total = total + arrived[i]
    for i in range(copies.shape[0]):
        copies[i] = total


def parts_kernel(sums, done, depth_one, point_one, depth_two, point_two):
    for a in range(3):
        for b in range(3):
            row = 9 * a + 3 * b
            depth_one[a, b] = sums[row : row + 3, :]
            depth_two[a, b] = sums[160 + row : 163 + row, :]
    point_one[...] = sums[32:160, :]
    point_two[...] = sums[192:320, :]


def call(kernel, scratch, outs, flops, *args):
    vmem = pl.BlockSpec(memory_space=pltpu.VMEM)
    smem = pl.BlockSpec(memory_space=pltpu.SMEM)
    moved = sum(a.size * a.dtype.itemsize for a in args) + sum(
        o.size * o.dtype.itemsize for o in outs
    )
    return pl.pallas_call(
        kernel,
        out_shape=outs,
        in_specs=[smem if a.dtype == jnp.int32 else vmem for a in args],
        out_specs=[vmem] * len(outs),
        scratch_shapes=scratch,
        cost_estimate=pl.CostEstimate(flops=flops, bytes_accessed=moved, transcendentals=0),
        compiler_params=pltpu.CompilerParams(vmem_limit_bytes=VMEM_LIMIT),
    )(*args)


SPACE = ("outer", "ring", "core")
ACROSS = ("outer", "core", "dp")


def with_other_core(v):
    return lax.ppermute(v, "core", [(0, 1), (1, 0)])


def with_other_chip(v):
    count = math.prod(lax.axis_size(name) for name in SPACE)
    pairs = [(i, i + 1) for i in range(1, count - 1, 2)]
    return lax.ppermute(v, SPACE, pairs + [(j, i) for i, j in pairs])


def reduced_across(terms):
    count = math.prod(lax.axis_size(name) for name in ACROSS)
    tiles = terms.reshape(count, 1, -1)
    return lax.all_to_all(tiles, ACROSS, 0, 0, tiled=True).sum(axis=0)


def reduced_around(share):
    copies = jnp.broadcast_to(share, (lax.axis_size("ring"), *share.shape))
    arrived = lax.all_to_all(copies, "ring", 0, 0, tiled=True)
    count = math.prod(lax.axis_size(name) for name in ACROSS)
    (copies,) = call(
        sum_kernel, [], [jax.ShapeDtypeStruct((count, *share.shape), share.dtype)], 0, arrived
    )
    return copies


def gathered_across(copies):
    return lax.all_to_all(copies, ACROSS, 0, 0, tiled=True).reshape(TERMS, CH)


def on_device(inputs, depth_one, point_one, depth_two, point_two, cotangent):
    f32, bf16 = jnp.float32, jnp.bfloat16
    shape = jax.ShapeDtypeStruct
    block_in = inputs.reshape(2, CELLS, CH)
    block_up = cotangent.reshape(2, CELLS, CH)
    d1 = depth_one.reshape(27, CH)
    d2 = depth_two.reshape(27, CH)
    core = lax.axis_index("core")
    parity = core.astype(jnp.int32).reshape(1)


    def both(x):
        return jnp.concatenate(
            [lax.dynamic_slice_in_dim(block, x, 1, 0) for block in (block_in, block_up)], axis=0
        )

    outer = both(core)
    outer, inner = lax.optimization_barrier((outer, 1 - core))
    far = with_other_chip(outer)
    near = with_other_core(both(inner))
    slots = pltpu.VMEM((4, PADDED, CH), bf16)
    local_w = pltpu.VMEM((6 * CH, 6 * CH), bf16)
    side_w = pltpu.VMEM((4 * CH, 6 * CH), bf16)
    flipped = pltpu.VMEM((3 * CH, CELLS), bf16)
    totals = pltpu.VMEM((3, CH, CH), f32)
    devices = math.prod(lax.axis_size(name) for name in ("dp", *SPACE))
    factor = 1.0 / math.sqrt(devices * 2 * CELLS)
    local_one, local_two, side_one, side_two, far_w1, far_w2 = call(
        taps_kernel,
        [],
        [shape((6 * CH, 6 * CH), bf16)] * 2 + [shape((4 * CH, 6 * CH), bf16)] * 4,
        1_000_000_000,
        parity, d1, point_one, d2, point_two,
    )
    inner, pre, carried, terms = call(
        functools.partial(near_kernel, factor),
        [slots, slots, flipped, flipped, totals],
        [shape((CELLS, CH), bf16)] + [shape((CELLS, CH), f32)] * 2 + [shape((TERMS, CH), f32)],
        6_000_000_000,
        parity, block_in, block_up, near, local_one, local_two, side_one, side_two,
        d1, point_one, d2, point_two,
    )
    outer, terms = call(
        functools.partial(far_kernel, factor),
        [slots, slots, flipped, flipped, totals],
        [shape((CELLS, CH), bf16), shape((TERMS, CH), f32)],
        4_000_000_000,
        parity, block_in, block_up, far, pre, carried, far_w1, far_w2,
        d1, point_one, d2, point_two, terms,
    )
    copies = reduced_around(reduced_across(terms))
    copies, inner, outer = lax.optimization_barrier((copies, inner, outer))
    outer_beside = with_other_chip(outer)
    inner_beside = with_other_core(inner)
    grad, done = call(
        last_kernel,
        [slots, local_w, side_w, side_w],
        [shape((2, CELLS, CH), bf16), shape((8, CH), f32)],
        4_000_000_000,
        parity, inner, outer, inner_beside, outer_beside, d1, point_one,
    )
    sums = gathered_across(copies)
    depth, point = (shape((3, 3, 3, CH), f32), shape((CH, CH), f32))
    parts = call(parts_kernel, [], [depth, point, depth, point], 0, sums, done)
    return (grad.reshape(inputs.shape), *parts)


def solution(mesh):
    count, samples = (mesh.shape["space"], mesh.shape["dp"])
    ring = min(8, count // 2)
    grid = mesh.devices.reshape(count // (2 * ring), ring, 2, samples)
    split = jax.sharding.Mesh(grid, (*SPACE, "dp"))
    slabs = P("dp", SPACE, None, None, None, None)
    return jax.shard_map(
        on_device,
        mesh=split,
        in_specs=(slabs, P(), P(), P(), P(), slabs),
        out_specs=(slabs, P(), P(), P(), P()),
        check_vma=False,
    )
```

```python
import functools
import math

import jax
import jax.numpy as jnp
from jax import lax
from jax.experimental import pallas as pl
from jax.experimental.pallas import tpu as pltpu
from jax.sharding import PartitionSpec as P

CH = 128
LINE = 64
CELLS = 1024
PADDED = CELLS + 2 * LINE
ROWS = 256
TERMS = 320
VMEM_LIMIT = 24 * 1024 * 1024


def mm(a, b):
    return jnp.dot(a, b, preferred_element_type=jnp.float32)


def keep_mask(count, edge):
    return lax.broadcasted_iota(jnp.int32, (count, 1), 0) % LINE != edge


def from_before(v):
    return jnp.where(keep_mask(v.shape[0], 0), pltpu.roll(v, 1, 0), 0.0)


def from_after(v):
    return jnp.where(keep_mask(v.shape[0], LINE - 1), pltpu.roll(v, v.shape[0] - 1, 0), 0.0)


def shift_sum(products, width):
    return (
        from_before(products[:, :width])
        + products[:, width : 2 * width]
        + from_after(products[:, 2 * width :])
    )


def set_plane(ref, slot, plane):
    edge = jnp.zeros((LINE, CH), jnp.bfloat16)
    ref[slot, 0:LINE, :] = edge
    ref[slot, LINE : LINE + CELLS, :] = plane
    ref[slot, LINE + CELLS : PADDED, :] = edge


def local_products(planes, weights, start):
    left = jnp.concatenate(
        [
            planes[1 + p, start + b * LINE : start + b * LINE + ROWS, :]
            for p in range(2)
            for b in range(3)
        ],
        axis=1,
    )
    return shift_sum(mm(left, weights[...]), 2 * CH)


def side_products(planes, slot, weights, start):
    pairs = ROWS // LINE
    left = jnp.concatenate(
        [
            jnp.concatenate(
                [
                    planes[slot, start + (2 * j + i) * LINE : start + (2 * j + i + 1) * LINE, :]
                    for j in range(pairs)
                ],
                axis=0,
            )
            for i in range(4)
        ],
        axis=1,
    )
    out = shift_sum(mm(left, weights[...]), 2 * CH)
    return jnp.concatenate(
        [
            out[j * LINE : (j + 1) * LINE, q * CH : (q + 1) * CH]
            for j in range(pairs)
            for q in range(2)
        ],
        axis=0,
    )


def fill_local(ref, tap_matrix):
    for a in range(3):
        for b in range(3):
            for e in range(3):
                block = tap_matrix(9 * a + 3 * b + e)
                for p in range(2):
                    x = p + 1 - a
                    if 0 <= x < 2:
                        row, col = ((3 * p + b) * CH, (2 * e + x) * CH)
                        ref[row : row + CH, col : col + CH] = block


def fill_side(ref, tap_matrix, high):
    ref[...] = jnp.zeros(ref.shape, jnp.bfloat16)
    for b in range(3):
        for e in range(3):
            block = jnp.where(high, tap_matrix(18 + 3 * b + e), tap_matrix(3 * b + e))
            for q in range(2):
                row, col = ((b + q) * CH, (2 * e + q) * CH)
                ref[row : row + CH, col : col + CH] = block


def columns_of(depth):
    padded = jnp.concatenate([depth, jnp.zeros((CH - 27, CH), jnp.float32)], axis=0)
    return padded.T


def forward_taps(cols, point):
    return lambda s: (cols[:, s : s + 1] * point).astype(jnp.bfloat16)


def backward_taps(depth, point_t):
    return lambda s: (depth[26 - s : 27 - s, :] * point_t).astype(jnp.bfloat16)


def tap_sums(left_t, planes, x, combine):
    order = [(a, b) for a in range(3) for b in range(3)]
    for at in range(0, 9, 2):
        group = order[at : at + 2]
        right = jnp.concatenate(
            [planes[x + a, b * LINE : b * LINE + CELLS, :] for a, b in group], axis=1
        )
        sums = mm(left_t[...], right)
        for i, (a, b) in enumerate(group):
            for e in range(3):
                combine(9 * a + 3 * b + e, sums[e * CH : (e + 1) * CH, i * CH : (i + 1) * CH])


def activate(value, back, scaled_out, scaled_t, hidden_t, start):
    sigma = jax.nn.sigmoid(value)
    hidden = (value * sigma).astype(jnp.bfloat16).astype(jnp.float32)
    scaled = (back * (sigma * (1.0 + value * (1.0 - sigma)))).astype(jnp.bfloat16)
    scaled_out[start : start + ROWS, :] = scaled
    scaled = scaled.astype(jnp.float32)
    for ref, v in ((scaled_t, scaled), (hidden_t, hidden)):
        shifted = jnp.concatenate([from_after(v), v, from_before(v)], axis=1)
        ref[:, start : start + ROWS] = shifted.astype(jnp.bfloat16).T


def weight_terms(factor, x, planes_in, planes_up, scaled_t, hidden_t, weights, total, before, terms):
    depth_one, point_one, depth_two, point_two = weights
    point_one_t = point_one.T
    cols_two = columns_of(depth_two)
    lane = lax.broadcasted_iota(jnp.int32, (CH, CH), 1)
    total[...] = jnp.zeros((3, CH, CH), jnp.float32)
    terms[...] = jnp.zeros((TERMS, CH), jnp.float32) if before is None else before[...]

    def layer_one(s, block):
        total[0] += depth_one[s : s + 1, :] * block
        terms[s : s + 1, :] += jnp.sum(point_one_t * block, axis=0, keepdims=True) * factor

    tap_sums(scaled_t, planes_in, x, layer_one)
    terms[32:160, :] += total[0].T * factor

    def layer_two(s, block):
        s = 26 - s
        total[1] += cols_two[:, s : s + 1] * block
        total[2] += jnp.where(lane == s, jnp.sum(point_two * block, axis=1, keepdims=True), 0.0)

    tap_sums(hidden_t, planes_up, x, layer_two)
    terms[192:320, :] += total[1] * factor
    terms[160:192, :] += total[2].T[:32, :] * factor


def place_planes(planes, block, core, near, far):
    for x in range(2):
        set_plane(planes, 1 + x, block[x])
    if near is not None:
        set_plane(planes, 3 - 3 * core, near)
    if far is not None:
        set_plane(planes, 3 * core, far)


def taps_kernel(
    parity, d1, p1, d2, p2, local_one, local_two, side_one, side_two, far_w1, far_w2
):
    near_high = parity[0] == 0
    depth_one, point_one, depth_two, point_two = (
        w[...].astype(jnp.float32) for w in (d1, p1, d2, p2)
    )
    taps_one = forward_taps(columns_of(depth_one), point_one)
    taps_two = backward_taps(depth_two, point_two.T)
    for taps, local, side, other in (
        (taps_one, local_one, side_one, far_w1),
        (taps_two, local_two, side_two, far_w2),
    ):
        fill_local(local, taps)
        fill_side(side, taps, near_high)
        fill_side(other, taps, jnp.logical_not(near_high))


def near_kernel(
    factor,
    parity, block_in, block_up, near, local_one, local_two, side_one, side_two, d1, p1, d2, p2,
    scaled_out, pre, carried, terms,
    planes_in, planes_up, scaled_t, hidden_t, total,
):
    core = parity[0]
    inner = 1 - core
    weights = tuple(w[...].astype(jnp.float32) for w in (d1, p1, d2, p2))
    place_planes(planes_in, block_in, core, near[0], None)
    place_planes(planes_up, block_up, core, near[1], None)
    near_high = core == 0
    near_slot = 3 - 3 * core
    for half in range(0, CELLS, 2 * ROWS):
        side_in = side_products(planes_in, near_slot, side_one, half)
        side_up = side_products(planes_up, near_slot, side_two, half)
        for at in range(0, 2 * ROWS, ROWS):
            start = half + at
            both_in = local_products(planes_in, local_one, start)
            both_up = local_products(planes_up, local_two, start)
            low, high = (both_in[:, :CH], both_in[:, CH:])
            pre[start : start + ROWS, :] = jnp.where(near_high, low, high)
            value = jnp.where(near_high, high, low) + side_in[at : at + ROWS, :]
            low, high = (both_up[:, :CH], both_up[:, CH:])
            carried[start : start + ROWS, :] = jnp.where(near_high, low, high)
            back = jnp.where(near_high, high, low) + side_up[at : at + ROWS, :]
            activate(value, back, scaled_out, scaled_t, hidden_t, start)
    weight_terms(
        factor, inner, planes_in, planes_up, scaled_t, hidden_t, weights, total, None, terms
    )


def far_kernel(
    factor,
    parity, block_in, block_up, far, pre, carried, far_w1, far_w2, d1, p1, d2, p2, before,
    scaled_out, terms,
    planes_in, planes_up, scaled_t, hidden_t, total,
):
    core = parity[0]
    weights = tuple(w[...].astype(jnp.float32) for w in (d1, p1, d2, p2))
    place_planes(planes_in, block_in, core, None, far[0])
    place_planes(planes_up, block_up, core, None, far[1])
    for half in range(0, CELLS, 2 * ROWS):
        side_in = side_products(planes_in, 3 * core, far_w1, half)
        side_up = side_products(planes_up, 3 * core, far_w2, half)
        for at in range(0, 2 * ROWS, ROWS):
            start = half + at
            value = side_in[at : at + ROWS, :] + pre[start : start + ROWS, :]
            back = side_up[at : at + ROWS, :] + carried[start : start + ROWS, :]
            activate(value, back, scaled_out, scaled_t, hidden_t, start)
    weight_terms(
        factor, core, planes_in, planes_up, scaled_t, hidden_t, weights, total, before, terms
    )


def own_kernel(parity, inner, outer, d1, p1, out, planes, local):
    core = parity[0]
    depth_one = d1[...].astype(jnp.float32)
    fill_local(local, backward_taps(depth_one, p1[...].astype(jnp.float32).T))
    set_plane(planes, 2 - core, inner[...])
    set_plane(planes, 1 + core, outer[...])
    for start in range(0, CELLS, ROWS):
        both = local_products(planes, local, start)
        out[0, start : start + ROWS, :] = both[:, :CH]
        out[1, start : start + ROWS, :] = both[:, CH:]


def last_kernel(parity, own, near, far, d1, p1, out, done, planes, low_side, high_side):
    core = parity[0]
    depth_one = d1[...].astype(jnp.float32)
    taps = backward_taps(depth_one, p1[...].astype(jnp.float32).T)
    fill_side(low_side, taps, False)
    fill_side(high_side, taps, True)
    set_plane(planes, 1 - core, near[...])
    set_plane(planes, core, far[...])
    for start in range(0, CELLS, 2 * ROWS):
        rows = slice(start, start + 2 * ROWS)
        low = side_products(planes, 0, low_side, start)
        out[0, rows, :] = (own[0, rows, :] + low).astype(jnp.bfloat16)
        high = side_products(planes, 1, high_side, start)
        out[1, rows, :] = (own[1, rows, :] + high).astype(jnp.bfloat16)
    done[...] = jnp.zeros((8, CH), jnp.float32)


def sum_kernel(arrived, copies):
    total = arrived[0]
    for i in range(1, arrived.shape[0]):
        total = total + arrived[i]
    for i in range(copies.shape[0]):
        copies[i] = total


def parts_kernel(sums, done, depth_one, point_one, depth_two, point_two):
    for a in range(3):
        for b in range(3):
            row = 9 * a + 3 * b
            depth_one[a, b] = sums[row : row + 3, :]
            depth_two[a, b] = sums[160 + row : 163 + row, :]
    point_one[...] = sums[32:160, :]
    point_two[...] = sums[192:320, :]


def call(kernel, scratch, outs, flops, *args):
    vmem = pl.BlockSpec(memory_space=pltpu.VMEM)
    smem = pl.BlockSpec(memory_space=pltpu.SMEM)
    moved = sum(a.size * a.dtype.itemsize for a in args) + sum(
        o.size * o.dtype.itemsize for o in outs
    )
    return pl.pallas_call(
        kernel,
        out_shape=outs,
        in_specs=[smem if a.dtype == jnp.int32 else vmem for a in args],
        out_specs=[vmem] * len(outs),
        scratch_shapes=scratch,
        cost_estimate=pl.CostEstimate(flops=flops, bytes_accessed=moved, transcendentals=0),
        compiler_params=pltpu.CompilerParams(vmem_limit_bytes=VMEM_LIMIT),
    )(*args)


SPACE = ("outer", "ring", "core")
ACROSS = ("outer", "core", "dp")


def with_other_core(v):
    return lax.ppermute(v, "core", [(0, 1), (1, 0)])


def with_other_chip(v):
    count = math.prod(lax.axis_size(name) for name in SPACE)
    pairs = [(i, i + 1) for i in range(1, count - 1, 2)]
    return lax.ppermute(v, SPACE, pairs + [(j, i) for i, j in pairs])


def reduced_across(terms):
    count = math.prod(lax.axis_size(name) for name in ACROSS)
    tiles = terms.reshape(count, 1, -1)
    return lax.all_to_all(tiles, ACROSS, 0, 0, tiled=True).sum(axis=0)


def reduced_around(share):
    copies = jnp.broadcast_to(share, (lax.axis_size("ring"), *share.shape))
    arrived = lax.all_to_all(copies, "ring", 0, 0, tiled=True)
    count = math.prod(lax.axis_size(name) for name in ACROSS)
    (copies,) = call(
        sum_kernel, [], [jax.ShapeDtypeStruct((count, *share.shape), share.dtype)], 0, arrived
    )
    return copies


def gathered_across(copies):
    return lax.all_to_all(copies, ACROSS, 0, 0, tiled=True).reshape(TERMS, CH)


def on_device(inputs, depth_one, point_one, depth_two, point_two, cotangent):
    f32, bf16 = jnp.float32, jnp.bfloat16
    shape = jax.ShapeDtypeStruct
    block_in = inputs.reshape(2, CELLS, CH)
    block_up = cotangent.reshape(2, CELLS, CH)
    d1 = depth_one.reshape(27, CH)
    d2 = depth_two.reshape(27, CH)
    core = lax.axis_index("core")
    parity = core.astype(jnp.int32).reshape(1)


    def both(x):
        return jnp.concatenate(
            [lax.dynamic_slice_in_dim(block, x, 1, 0) for block in (block_in, block_up)], axis=0
        )

    outer = both(core)
    outer, inner = lax.optimization_barrier((outer, 1 - core))
    far = with_other_chip(outer)
    near = with_other_core(both(inner))
    slots = pltpu.VMEM((4, PADDED, CH), bf16)
    local_w = pltpu.VMEM((6 * CH, 6 * CH), bf16)
    side_w = pltpu.VMEM((4 * CH, 6 * CH), bf16)
    flipped = pltpu.VMEM((3 * CH, CELLS), bf16)
    totals = pltpu.VMEM((3, CH, CH), f32)
    devices = math.prod(lax.axis_size(name) for name in ("dp", *SPACE))
    factor = 1.0 / math.sqrt(devices * 2 * CELLS)
    local_one, local_two, side_one, side_two, far_w1, far_w2 = call(
        taps_kernel,
        [],
        [shape((6 * CH, 6 * CH), bf16)] * 2 + [shape((4 * CH, 6 * CH), bf16)] * 4,
        1_000_000_000,
        parity, d1, point_one, d2, point_two,
    )
    inner, pre, carried, terms = call(
        functools.partial(near_kernel, factor),
        [slots, slots, flipped, flipped, totals],
        [shape((CELLS, CH), bf16)] + [shape((CELLS, CH), f32)] * 2 + [shape((TERMS, CH), f32)],
        6_000_000_000,
        parity, block_in, block_up, near, local_one, local_two, side_one, side_two,
        d1, point_one, d2, point_two,
    )
    outer, terms = call(
        functools.partial(far_kernel, factor),
        [slots, slots, flipped, flipped, totals],
        [shape((CELLS, CH), bf16), shape((TERMS, CH), f32)],
        4_000_000_000,
        parity, block_in, block_up, far, pre, carried, far_w1, far_w2,
        d1, point_one, d2, point_two, terms,
    )
    share = reduced_across(terms)
    outer_beside = with_other_chip(outer)
    inner_beside = with_other_core(inner)
    (own,) = call(
        own_kernel,
        [slots, local_w],
        [shape((2, CELLS, CH), f32)],
        8_000_000_000,
        parity, inner, outer, d1, point_one,
    )
    grad, done = call(
        last_kernel,
        [pltpu.VMEM((2, PADDED, CH), bf16), side_w, side_w],
        [shape((2, CELLS, CH), bf16), shape((8, CH), f32)],
        2_000_000_000,
        parity, own, inner_beside, outer_beside, d1, point_one,
    )
    sums = gathered_across(reduced_around(share))
    depth, point = (shape((3, 3, 3, CH), f32), shape((CH, CH), f32))
    parts = call(parts_kernel, [], [depth, point, depth, point], 0, sums, done)
    return (grad.reshape(inputs.shape), *parts)


def solution(mesh):
    count, samples = (mesh.shape["space"], mesh.shape["dp"])
    ring = min(8, count // 2)
    grid = mesh.devices.reshape(count // (2 * ring), ring, 2, samples)
    split = jax.sharding.Mesh(grid, (*SPACE, "dp"))
    slabs = P("dp", SPACE, None, None, None, None)
    return jax.shard_map(
        on_device,
        mesh=split,
        in_specs=(slabs, P(), P(), P(), P(), slabs),
        out_specs=(slabs, P(), P(), P(), P()),
        check_vma=False,
    )
```

```python
import functools
import math

import jax
import jax.numpy as jnp
from jax import lax
from jax.experimental import pallas as pl
from jax.experimental.pallas import tpu as pltpu
from jax.sharding import PartitionSpec as P

CH = 128
LINE = 64
CELLS = 1024
PADDED = CELLS + 2 * LINE
ROWS = 256
TERMS = 320
VMEM_LIMIT = 24 * 1024 * 1024


def mm(a, b):
    return jnp.dot(a, b, preferred_element_type=jnp.float32)


def keep_mask(count, edge):
    return lax.broadcasted_iota(jnp.int32, (count, 1), 0) % LINE != edge


def from_before(v):
    return jnp.where(keep_mask(v.shape[0], 0), pltpu.roll(v, 1, 0), 0.0)


def from_after(v):
    return jnp.where(keep_mask(v.shape[0], LINE - 1), pltpu.roll(v, v.shape[0] - 1, 0), 0.0)


def shift_sum(products, width):
    return (
        from_before(products[:, :width])
        + products[:, width : 2 * width]
        + from_after(products[:, 2 * width :])
    )


def set_plane(ref, slot, plane):
    edge = jnp.zeros((LINE, CH), jnp.bfloat16)
    ref[slot, 0:LINE, :] = edge
    ref[slot, LINE : LINE + CELLS, :] = plane
    ref[slot, LINE + CELLS : PADDED, :] = edge


def local_products(planes, weights, start):
    left = jnp.concatenate(
        [
            planes[1 + p, start + b * LINE : start + b * LINE + ROWS, :]
            for p in range(2)
            for b in range(3)
        ],
        axis=1,
    )
    return shift_sum(mm(left, weights[...]), 2 * CH)


def side_products(planes, slot, weights, start):
    pairs = ROWS // LINE
    left = jnp.concatenate(
        [
            jnp.concatenate(
                [
                    planes[slot, start + (2 * j + i) * LINE : start + (2 * j + i + 1) * LINE, :]
                    for j in range(pairs)
                ],
                axis=0,
            )
            for i in range(4)
        ],
        axis=1,
    )
    out = shift_sum(mm(left, weights[...]), 2 * CH)
    return jnp.concatenate(
        [
            out[j * LINE : (j + 1) * LINE, q * CH : (q + 1) * CH]
            for j in range(pairs)
            for q in range(2)
        ],
        axis=0,
    )


def fill_local(ref, tap_matrix):
    for a in range(3):
        for b in range(3):
            for e in range(3):
                block = tap_matrix(9 * a + 3 * b + e)
                for p in range(2):
                    x = p + 1 - a
                    if 0 <= x < 2:
                        row, col = ((3 * p + b) * CH, (2 * e + x) * CH)
                        ref[row : row + CH, col : col + CH] = block


def fill_side(ref, tap_matrix, high):
    ref[...] = jnp.zeros(ref.shape, jnp.bfloat16)
    for b in range(3):
        for e in range(3):
            block = jnp.where(high, tap_matrix(18 + 3 * b + e), tap_matrix(3 * b + e))
            for q in range(2):
                row, col = ((b + q) * CH, (2 * e + q) * CH)
                ref[row : row + CH, col : col + CH] = block


def columns_of(depth):
    padded = jnp.concatenate([depth, jnp.zeros((CH - 27, CH), jnp.float32)], axis=0)
    return padded.T


def forward_taps(cols, point):
    return lambda s: (cols[:, s : s + 1] * point).astype(jnp.bfloat16)


def backward_taps(depth, point_t):
    return lambda s: (depth[26 - s : 27 - s, :] * point_t).astype(jnp.bfloat16)


def tap_sums(left_t, planes, x, combine):
    order = [(a, b) for a in range(3) for b in range(3)]
    for at in range(0, 9, 2):
        group = order[at : at + 2]
        right = jnp.concatenate(
            [planes[x + a, b * LINE : b * LINE + CELLS, :] for a, b in group], axis=1
        )
        sums = mm(left_t[...], right)
        for i, (a, b) in enumerate(group):
            for e in range(3):
                combine(9 * a + 3 * b + e, sums[e * CH : (e + 1) * CH, i * CH : (i + 1) * CH])


def activate(value, back, scaled_out, scaled_t, hidden_t, start):
    sigma = jax.nn.sigmoid(value)
    hidden = (value * sigma).astype(jnp.bfloat16).astype(jnp.float32)
    scaled = (back * (sigma * (1.0 + value * (1.0 - sigma)))).astype(jnp.bfloat16)
    scaled_out[start : start + ROWS, :] = scaled
    scaled = scaled.astype(jnp.float32)
    for ref, v in ((scaled_t, scaled), (hidden_t, hidden)):
        shifted = jnp.concatenate([from_after(v), v, from_before(v)], axis=1)
        ref[:, start : start + ROWS] = shifted.astype(jnp.bfloat16).T


def weight_terms(factor, x, planes_in, planes_up, scaled_t, hidden_t, weights, total, before, terms):
    depth_one, point_one, depth_two, point_two = weights
    point_one_t = point_one.T
    cols_two = columns_of(depth_two)
    lane = lax.broadcasted_iota(jnp.int32, (CH, CH), 1)
    total[...] = jnp.zeros((3, CH, CH), jnp.float32)
    terms[...] = jnp.zeros((TERMS, CH), jnp.float32) if before is None else before[...]

    def layer_one(s, block):
        total[0] += depth_one[s : s + 1, :] * block
        terms[s : s + 1, :] += jnp.sum(point_one_t * block, axis=0, keepdims=True) * factor

    tap_sums(scaled_t, planes_in, x, layer_one)
    terms[32:160, :] += total[0].T * factor

    def layer_two(s, block):
        s = 26 - s
        total[1] += cols_two[:, s : s + 1] * block
        total[2] += jnp.where(lane == s, jnp.sum(point_two * block, axis=1, keepdims=True), 0.0)

    tap_sums(hidden_t, planes_up, x, layer_two)
    terms[192:320, :] += total[1] * factor
    terms[160:192, :] += total[2].T[:32, :] * factor


def place_planes(planes, block, core, near, far):
    for x in range(2):
        set_plane(planes, 1 + x, block[x])
    if near is not None:
        set_plane(planes, 3 - 3 * core, near)
    if far is not None:
        set_plane(planes, 3 * core, far)


def taps_kernel(
    parity, d1, p1, d2, p2, local_one, local_two, side_one, side_two, far_w1, far_w2
):
    near_high = parity[0] == 0
    depth_one, point_one, depth_two, point_two = (
        w[...].astype(jnp.float32) for w in (d1, p1, d2, p2)
    )
    taps_one = forward_taps(columns_of(depth_one), point_one)
    taps_two = backward_taps(depth_two, point_two.T)
    for taps, local, side, other in (
        (taps_one, local_one, side_one, far_w1),
        (taps_two, local_two, side_two, far_w2),
    ):
        fill_local(local, taps)
        fill_side(side, taps, near_high)
        fill_side(other, taps, jnp.logical_not(near_high))


def near_kernel(
    factor,
    parity, block_in, block_up, near, local_one, local_two, side_one, side_two, d1, p1, d2, p2,
    scaled_out, pre, carried, terms,
    planes_in, planes_up, scaled_t, hidden_t, total,
):
    core = parity[0]
    inner = 1 - core
    weights = tuple(w[...].astype(jnp.float32) for w in (d1, p1, d2, p2))
    place_planes(planes_in, block_in, core, near[0], None)
    place_planes(planes_up, block_up, core, near[1], None)
    near_high = core == 0
    near_slot = 3 - 3 * core
    for half in range(0, CELLS, 2 * ROWS):
        side_in = side_products(planes_in, near_slot, side_one, half)
        side_up = side_products(planes_up, near_slot, side_two, half)
        for at in range(0, 2 * ROWS, ROWS):
            start = half + at
            both_in = local_products(planes_in, local_one, start)
            both_up = local_products(planes_up, local_two, start)
            low, high = (both_in[:, :CH], both_in[:, CH:])
            pre[start : start + ROWS, :] = jnp.where(near_high, low, high)
            value = jnp.where(near_high, high, low) + side_in[at : at + ROWS, :]
            low, high = (both_up[:, :CH], both_up[:, CH:])
            carried[start : start + ROWS, :] = jnp.where(near_high, low, high)
            back = jnp.where(near_high, high, low) + side_up[at : at + ROWS, :]
            activate(value, back, scaled_out, scaled_t, hidden_t, start)
    weight_terms(
        factor, inner, planes_in, planes_up, scaled_t, hidden_t, weights, total, None, terms
    )


def far_kernel(
    factor,
    parity, block_in, block_up, far, pre, carried, far_w1, far_w2, d1, p1, d2, p2, before,
    scaled_out, terms,
    planes_in, planes_up, scaled_t, hidden_t, total,
):
    core = parity[0]
    weights = tuple(w[...].astype(jnp.float32) for w in (d1, p1, d2, p2))
    place_planes(planes_in, block_in, core, None, far[0])
    place_planes(planes_up, block_up, core, None, far[1])
    for half in range(0, CELLS, 2 * ROWS):
        side_in = side_products(planes_in, 3 * core, far_w1, half)
        side_up = side_products(planes_up, 3 * core, far_w2, half)
        for at in range(0, 2 * ROWS, ROWS):
            start = half + at
            value = side_in[at : at + ROWS, :] + pre[start : start + ROWS, :]
            back = side_up[at : at + ROWS, :] + carried[start : start + ROWS, :]
            activate(value, back, scaled_out, scaled_t, hidden_t, start)
    weight_terms(
        factor, core, planes_in, planes_up, scaled_t, hidden_t, weights, total, before, terms
    )


def own_kernel(parity, inner, outer, d1, p1, out, planes, local):
    core = parity[0]
    depth_one = d1[...].astype(jnp.float32)
    fill_local(local, backward_taps(depth_one, p1[...].astype(jnp.float32).T))
    set_plane(planes, 2 - core, inner[...])
    set_plane(planes, 1 + core, outer[...])
    for start in range(0, CELLS, ROWS):
        both = local_products(planes, local, start)
        out[0, start : start + ROWS, :] = both[:, :CH]
        out[1, start : start + ROWS, :] = both[:, CH:]


def last_kernel(parity, own, near, far, d1, p1, out, done, planes, low_side, high_side):
    core = parity[0]
    depth_one = d1[...].astype(jnp.float32)
    taps = backward_taps(depth_one, p1[...].astype(jnp.float32).T)
    fill_side(low_side, taps, False)
    fill_side(high_side, taps, True)
    set_plane(planes, 1 - core, near[...])
    set_plane(planes, core, far[...])
    for start in range(0, CELLS, 2 * ROWS):
        rows = slice(start, start + 2 * ROWS)
        low = side_products(planes, 0, low_side, start)
        out[0, rows, :] = (own[0, rows, :] + low).astype(jnp.bfloat16)
        high = side_products(planes, 1, high_side, start)
        out[1, rows, :] = (own[1, rows, :] + high).astype(jnp.bfloat16)
    done[...] = jnp.zeros((8, CH), jnp.float32)


def sum_kernel(arrived, copies):
    total = arrived[0]
    for i in range(1, arrived.shape[0]):
        total = total + arrived[i]
    for i in range(copies.shape[0]):
        copies[i] = total


def parts_kernel(sums, done, depth_one, point_one, depth_two, point_two):
    for a in range(3):
        for b in range(3):
            row = 9 * a + 3 * b
            depth_one[a, b] = sums[row : row + 3, :]
            depth_two[a, b] = sums[160 + row : 163 + row, :]
    point_one[...] = sums[32:160, :]
    point_two[...] = sums[192:320, :]


def call(kernel, scratch, outs, flops, *args):
    vmem = pl.BlockSpec(memory_space=pltpu.VMEM)
    smem = pl.BlockSpec(memory_space=pltpu.SMEM)
    moved = sum(a.size * a.dtype.itemsize for a in args) + sum(
        o.size * o.dtype.itemsize for o in outs
    )
    return pl.pallas_call(
        kernel,
        out_shape=outs,
        in_specs=[smem if a.dtype == jnp.int32 else vmem for a in args],
        out_specs=[vmem] * len(outs),
        scratch_shapes=scratch,
        cost_estimate=pl.CostEstimate(flops=flops, bytes_accessed=moved, transcendentals=0),
        compiler_params=pltpu.CompilerParams(vmem_limit_bytes=VMEM_LIMIT),
    )(*args)


SPACE = ("outer", "ring", "core")
ACROSS = ("outer", "core", "dp")


def with_other_core(v):
    return lax.ppermute(v, "core", [(0, 1), (1, 0)])


def with_other_chip(v):
    count = math.prod(lax.axis_size(name) for name in SPACE)
    pairs = [(i, i + 1) for i in range(1, count - 1, 2)]
    return lax.ppermute(v, SPACE, pairs + [(j, i) for i, j in pairs])


def reduced_across(terms):
    count = math.prod(lax.axis_size(name) for name in ACROSS)
    tiles = terms.reshape(count, 1, -1)
    return lax.all_to_all(tiles, ACROSS, 0, 0, tiled=True).sum(axis=0)


def reduced_around(share):
    copies = jnp.broadcast_to(share, (lax.axis_size("ring"), *share.shape))
    arrived = lax.all_to_all(copies, "ring", 0, 0, tiled=True)
    count = math.prod(lax.axis_size(name) for name in ACROSS)
    (copies,) = call(
        sum_kernel, [], [jax.ShapeDtypeStruct((count, *share.shape), share.dtype)], 0, arrived
    )
    return copies


def gathered_across(copies):
    return lax.all_to_all(copies, ACROSS, 0, 0, tiled=True).reshape(TERMS, CH)


def on_device(inputs, depth_one, point_one, depth_two, point_two, cotangent):
    f32, bf16 = jnp.float32, jnp.bfloat16
    shape = jax.ShapeDtypeStruct
    block_in = inputs.reshape(2, CELLS, CH)
    block_up = cotangent.reshape(2, CELLS, CH)
    d1 = depth_one.reshape(27, CH)
    d2 = depth_two.reshape(27, CH)
    core = lax.axis_index("core")
    parity = core.astype(jnp.int32).reshape(1)


    def both(x):
        return jnp.concatenate(
            [lax.dynamic_slice_in_dim(block, x, 1, 0) for block in (block_in, block_up)], axis=0
        )

    outer = both(core)
    outer, inner = lax.optimization_barrier((outer, 1 - core))
    far = with_other_chip(outer)
    near = with_other_core(both(inner))
    slots = pltpu.VMEM((4, PADDED, CH), bf16)
    local_w = pltpu.VMEM((6 * CH, 6 * CH), bf16)
    side_w = pltpu.VMEM((4 * CH, 6 * CH), bf16)
    flipped = pltpu.VMEM((3 * CH, CELLS), bf16)
    totals = pltpu.VMEM((3, CH, CH), f32)
    devices = math.prod(lax.axis_size(name) for name in ("dp", *SPACE))
    factor = 1.0 / math.sqrt(devices * 2 * CELLS)
    local_one, local_two, side_one, side_two, far_w1, far_w2 = call(
        taps_kernel,
        [],
        [shape((6 * CH, 6 * CH), bf16)] * 2 + [shape((4 * CH, 6 * CH), bf16)] * 4,
        1_000_000_000,
        parity, d1, point_one, d2, point_two,
    )
    inner, pre, carried, terms = call(
        functools.partial(near_kernel, factor),
        [slots, slots, flipped, flipped, totals],
        [shape((CELLS, CH), bf16)] + [shape((CELLS, CH), f32)] * 2 + [shape((TERMS, CH), f32)],
        6_000_000_000,
        parity, block_in, block_up, near, local_one, local_two, side_one, side_two,
        d1, point_one, d2, point_two,
    )
    outer, terms = call(
        functools.partial(far_kernel, factor),
        [slots, slots, flipped, flipped, totals],
        [shape((CELLS, CH), bf16), shape((TERMS, CH), f32)],
        4_000_000_000,
        parity, block_in, block_up, far, pre, carried, far_w1, far_w2,
        d1, point_one, d2, point_two, terms,
    )
    share = reduced_across(terms)
    outer_beside = with_other_chip(outer)
    inner_beside = with_other_core(inner)
    copies = reduced_around(share)
    copies, own_inner, own_outer = lax.optimization_barrier((copies, inner, outer))
    (own,) = call(
        own_kernel,
        [slots, local_w],
        [shape((2, CELLS, CH), f32)],
        2_000_000_000,
        parity, own_inner, own_outer, d1, point_one,
    )
    grad, done = call(
        last_kernel,
        [pltpu.VMEM((2, PADDED, CH), bf16), side_w, side_w],
        [shape((2, CELLS, CH), bf16), shape((8, CH), f32)],
        2_000_000_000,
        parity, own, inner_beside, outer_beside, d1, point_one,
    )
    sums = gathered_across(copies)
    depth, point = (shape((3, 3, 3, CH), f32), shape((CH, CH), f32))
    parts = call(parts_kernel, [], [depth, point, depth, point], 0, sums, done)
    return (grad.reshape(inputs.shape), *parts)


def solution(mesh):
    count, samples = (mesh.shape["space"], mesh.shape["dp"])
    ring = min(8, count // 2)
    grid = mesh.devices.reshape(count // (2 * ring), ring, 2, samples)
    split = jax.sharding.Mesh(grid, (*SPACE, "dp"))
    slabs = P("dp", SPACE, None, None, None, None)
    return jax.shard_map(
        on_device,
        mesh=split,
        in_specs=(slabs, P(), P(), P(), P(), slabs),
        out_specs=(slabs, P(), P(), P(), P()),
        check_vma=False,
    )
```

```python
import functools
import math

import jax
import jax.numpy as jnp
from jax import lax
from jax.experimental import pallas as pl
from jax.experimental.pallas import tpu as pltpu
from jax.sharding import PartitionSpec as P

CH = 128
LINE = 64
CELLS = 1024
PADDED = CELLS + 2 * LINE
ROWS = 256
TERMS = 320
VMEM_LIMIT = 24 * 1024 * 1024


def mm(a, b):
    return jnp.dot(a, b, preferred_element_type=jnp.float32)


def keep_mask(count, edge):
    return lax.broadcasted_iota(jnp.int32, (count, 1), 0) % LINE != edge


def from_before(v):
    return jnp.where(keep_mask(v.shape[0], 0), pltpu.roll(v, 1, 0), 0.0)


def from_after(v):
    return jnp.where(keep_mask(v.shape[0], LINE - 1), pltpu.roll(v, v.shape[0] - 1, 0), 0.0)


def shift_sum(products, width):
    return (
        from_before(products[:, :width])
        + products[:, width : 2 * width]
        + from_after(products[:, 2 * width :])
    )


def set_plane(ref, slot, plane):
    edge = jnp.zeros((LINE, CH), jnp.bfloat16)
    ref[slot, 0:LINE, :] = edge
    ref[slot, LINE : LINE + CELLS, :] = plane
    ref[slot, LINE + CELLS : PADDED, :] = edge


def local_products(planes, weights, start):
    left = jnp.concatenate(
        [
            planes[1 + p, start + b * LINE : start + b * LINE + ROWS, :]
            for p in range(2)
            for b in range(3)
        ],
        axis=1,
    )
    return shift_sum(mm(left, weights[...]), 2 * CH)


def side_products(planes, slot, weights, start):
    pairs = ROWS // LINE
    left = jnp.concatenate(
        [
            jnp.concatenate(
                [
                    planes[slot, start + (2 * j + i) * LINE : start + (2 * j + i + 1) * LINE, :]
                    for j in range(pairs)
                ],
                axis=0,
            )
            for i in range(4)
        ],
        axis=1,
    )
    out = shift_sum(mm(left, weights[...]), 2 * CH)
    return jnp.concatenate(
        [
            out[j * LINE : (j + 1) * LINE, q * CH : (q + 1) * CH]
            for j in range(pairs)
            for q in range(2)
        ],
        axis=0,
    )


def fill_local(ref, tap_matrix):
    for a in range(3):
        for b in range(3):
            for e in range(3):
                block = tap_matrix(9 * a + 3 * b + e)
                for p in range(2):
                    x = p + 1 - a
                    if 0 <= x < 2:
                        row, col = ((3 * p + b) * CH, (2 * e + x) * CH)
                        ref[row : row + CH, col : col + CH] = block


def fill_side(ref, tap_matrix, high):
    ref[...] = jnp.zeros(ref.shape, jnp.bfloat16)
    for b in range(3):
        for e in range(3):
            block = jnp.where(high, tap_matrix(18 + 3 * b + e), tap_matrix(3 * b + e))
            for q in range(2):
                row, col = ((b + q) * CH, (2 * e + q) * CH)
                ref[row : row + CH, col : col + CH] = block


def columns_of(depth):
    padded = jnp.concatenate([depth, jnp.zeros((CH - 27, CH), jnp.float32)], axis=0)
    return padded.T


def forward_taps(cols, point):
    return lambda s: (cols[:, s : s + 1] * point).astype(jnp.bfloat16)


def backward_taps(depth, point_t):
    return lambda s: (depth[26 - s : 27 - s, :] * point_t).astype(jnp.bfloat16)


def tap_sums(left_t, planes, x, combine):
    order = [(a, b) for a in range(3) for b in range(3)]
    for at in range(0, 9, 2):
        group = order[at : at + 2]
        right = jnp.concatenate(
            [planes[x + a, b * LINE : b * LINE + CELLS, :] for a, b in group], axis=1
        )
        sums = mm(left_t[...], right)
        for i, (a, b) in enumerate(group):
            for e in range(3):
                combine(9 * a + 3 * b + e, sums[e * CH : (e + 1) * CH, i * CH : (i + 1) * CH])


def activate(value, back, scaled_out, scaled_t, hidden_t, start):
    sigma = jax.nn.sigmoid(value)
    hidden = (value * sigma).astype(jnp.bfloat16).astype(jnp.float32)
    scaled = (back * (sigma * (1.0 + value * (1.0 - sigma)))).astype(jnp.bfloat16)
    scaled_out[start : start + ROWS, :] = scaled
    scaled = scaled.astype(jnp.float32)
    for ref, v in ((scaled_t, scaled), (hidden_t, hidden)):
        shifted = jnp.concatenate([from_after(v), v, from_before(v)], axis=1)
        ref[:, start : start + ROWS] = shifted.astype(jnp.bfloat16).T


def weight_terms(factor, x, planes_in, planes_up, scaled_t, hidden_t, weights, total, before, terms):
    depth_one, point_one, depth_two, point_two = weights
    point_one_t = point_one.T
    cols_two = columns_of(depth_two)
    lane = lax.broadcasted_iota(jnp.int32, (CH, CH), 1)
    total[...] = jnp.zeros((3, CH, CH), jnp.float32)
    terms[...] = jnp.zeros((TERMS, CH), jnp.float32) if before is None else before[...]

    def layer_one(s, block):
        total[0] += depth_one[s : s + 1, :] * block
        terms[s : s + 1, :] += jnp.sum(point_one_t * block, axis=0, keepdims=True) * factor

    tap_sums(scaled_t, planes_in, x, layer_one)
    terms[32:160, :] += total[0].T * factor

    def layer_two(s, block):
        s = 26 - s
        total[1] += cols_two[:, s : s + 1] * block
        total[2] += jnp.where(lane == s, jnp.sum(point_two * block, axis=1, keepdims=True), 0.0)

    tap_sums(hidden_t, planes_up, x, layer_two)
    terms[192:320, :] += total[1] * factor
    terms[160:192, :] += total[2].T[:32, :] * factor


def place_planes(planes, block, core, near, far):
    for x in range(2):
        set_plane(planes, 1 + x, block[x])
    if near is not None:
        set_plane(planes, 3 - 3 * core, near)
    if far is not None:
        set_plane(planes, 3 * core, far)


def taps_kernel(
    parity, d1, p1, d2, p2, local_one, local_two, side_one, side_two, far_w1, far_w2
):
    near_high = parity[0] == 0
    depth_one, point_one, depth_two, point_two = (
        w[...].astype(jnp.float32) for w in (d1, p1, d2, p2)
    )
    taps_one = forward_taps(columns_of(depth_one), point_one)
    taps_two = backward_taps(depth_two, point_two.T)
    for taps, local, side, other in (
        (taps_one, local_one, side_one, far_w1),
        (taps_two, local_two, side_two, far_w2),
    ):
        fill_local(local, taps)
        fill_side(side, taps, near_high)
        fill_side(other, taps, jnp.logical_not(near_high))


def near_kernel(
    factor,
    parity, block_in, block_up, near, local_one, local_two, side_one, side_two, d1, p1, d2, p2,
    scaled_out, pre, carried, terms,
    planes_in, planes_up, scaled_t, hidden_t, total,
):
    core = parity[0]
    inner = 1 - core
    weights = tuple(w[...].astype(jnp.float32) for w in (d1, p1, d2, p2))
    place_planes(planes_in, block_in, core, near[0], None)
    place_planes(planes_up, block_up, core, near[1], None)
    near_high = core == 0
    near_slot = 3 - 3 * core
    for half in range(0, CELLS, 2 * ROWS):
        side_in = side_products(planes_in, near_slot, side_one, half)
        side_up = side_products(planes_up, near_slot, side_two, half)
        for at in range(0, 2 * ROWS, ROWS):
            start = half + at
            both_in = local_products(planes_in, local_one, start)
            both_up = local_products(planes_up, local_two, start)
            low, high = (both_in[:, :CH], both_in[:, CH:])
            pre[start : start + ROWS, :] = jnp.where(near_high, low, high)
            value = jnp.where(near_high, high, low) + side_in[at : at + ROWS, :]
            low, high = (both_up[:, :CH], both_up[:, CH:])
            carried[start : start + ROWS, :] = jnp.where(near_high, low, high)
            back = jnp.where(near_high, high, low) + side_up[at : at + ROWS, :]
            activate(value, back, scaled_out, scaled_t, hidden_t, start)
    weight_terms(
        factor, inner, planes_in, planes_up, scaled_t, hidden_t, weights, total, None, terms
    )


def far_kernel(
    factor,
    parity, block_in, block_up, far, pre, carried, far_w1, far_w2, d1, p1, d2, p2, before,
    scaled_out, terms,
    planes_in, planes_up, scaled_t, hidden_t, total,
):
    core = parity[0]
    weights = tuple(w[...].astype(jnp.float32) for w in (d1, p1, d2, p2))
    place_planes(planes_in, block_in, core, None, far[0])
    place_planes(planes_up, block_up, core, None, far[1])
    for half in range(0, CELLS, 2 * ROWS):
        side_in = side_products(planes_in, 3 * core, far_w1, half)
        side_up = side_products(planes_up, 3 * core, far_w2, half)
        for at in range(0, 2 * ROWS, ROWS):
            start = half + at
            value = side_in[at : at + ROWS, :] + pre[start : start + ROWS, :]
            back = side_up[at : at + ROWS, :] + carried[start : start + ROWS, :]
            activate(value, back, scaled_out, scaled_t, hidden_t, start)
    weight_terms(
        factor, core, planes_in, planes_up, scaled_t, hidden_t, weights, total, before, terms
    )


def own_kernel(parity, inner, outer, d1, p1, out, planes, local):
    core = parity[0]
    depth_one = d1[...].astype(jnp.float32)
    fill_local(local, backward_taps(depth_one, p1[...].astype(jnp.float32).T))
    set_plane(planes, 2 - core, inner[...])
    set_plane(planes, 1 + core, outer[...])
    for start in range(0, CELLS, ROWS):
        both = local_products(planes, local, start)
        out[0, start : start + ROWS, :] = both[:, :CH]
        out[1, start : start + ROWS, :] = both[:, CH:]


def last_kernel(parity, own, near, far, d1, p1, out, done, planes, low_side, high_side):
    core = parity[0]
    depth_one = d1[...].astype(jnp.float32)
    taps = backward_taps(depth_one, p1[...].astype(jnp.float32).T)
    fill_side(low_side, taps, False)
    fill_side(high_side, taps, True)
    set_plane(planes, 1 - core, near[...])
    set_plane(planes, core, far[...])
    for start in range(0, CELLS, 2 * ROWS):
        rows = slice(start, start + 2 * ROWS)
        low = side_products(planes, 0, low_side, start)
        out[0, rows, :] = (own[0, rows, :] + low).astype(jnp.bfloat16)
        high = side_products(planes, 1, high_side, start)
        out[1, rows, :] = (own[1, rows, :] + high).astype(jnp.bfloat16)
    done[...] = jnp.zeros((8, CH), jnp.float32)


def sum_kernel(arrived, copies):
    total = arrived[0]
    for i in range(1, arrived.shape[0]):
        total = total + arrived[i]
    for i in range(copies.shape[0]):
        copies[i] = total


def parts_kernel(sums, done, depth_one, point_one, depth_two, point_two):
    for a in range(3):
        for b in range(3):
            row = 9 * a + 3 * b
            depth_one[a, b] = sums[row : row + 3, :]
            depth_two[a, b] = sums[160 + row : 163 + row, :]
    point_one[...] = sums[32:160, :]
    point_two[...] = sums[192:320, :]


def call(kernel, scratch, outs, flops, *args):
    vmem = pl.BlockSpec(memory_space=pltpu.VMEM)
    smem = pl.BlockSpec(memory_space=pltpu.SMEM)
    moved = sum(a.size * a.dtype.itemsize for a in args) + sum(
        o.size * o.dtype.itemsize for o in outs
    )
    return pl.pallas_call(
        kernel,
        out_shape=outs,
        in_specs=[smem if a.dtype == jnp.int32 else vmem for a in args],
        out_specs=[vmem] * len(outs),
        scratch_shapes=scratch,
        cost_estimate=pl.CostEstimate(flops=flops, bytes_accessed=moved, transcendentals=0),
        compiler_params=pltpu.CompilerParams(vmem_limit_bytes=VMEM_LIMIT),
    )(*args)


SPACE = ("outer", "ring", "core")
ACROSS = ("outer", "core", "dp")


def with_other_core(v):
    return lax.ppermute(v, "core", [(0, 1), (1, 0)])


def with_other_chip(v):
    count = math.prod(lax.axis_size(name) for name in SPACE)
    pairs = [(i, i + 1) for i in range(1, count - 1, 2)]
    return lax.ppermute(v, SPACE, pairs + [(j, i) for i, j in pairs])


def reduced_across(terms):
    count = math.prod(lax.axis_size(name) for name in ACROSS)
    tiles = terms.reshape(count, 1, -1)
    return lax.all_to_all(tiles, ACROSS, 0, 0, tiled=True).sum(axis=0)


def reduced_around(share):
    copies = jnp.broadcast_to(share, (lax.axis_size("ring"), *share.shape))
    arrived = lax.all_to_all(copies, "ring", 0, 0, tiled=True)
    count = math.prod(lax.axis_size(name) for name in ACROSS)
    (copies,) = call(
        sum_kernel, [], [jax.ShapeDtypeStruct((count, *share.shape), share.dtype)], 0, arrived
    )
    return copies


def gathered_across(copies):
    return lax.all_to_all(copies, ACROSS, 0, 0, tiled=True).reshape(TERMS, CH)


def on_device(inputs, depth_one, point_one, depth_two, point_two, cotangent):
    f32, bf16 = jnp.float32, jnp.bfloat16
    shape = jax.ShapeDtypeStruct
    block_in = inputs.reshape(2, CELLS, CH)
    block_up = cotangent.reshape(2, CELLS, CH)
    d1 = depth_one.reshape(27, CH)
    d2 = depth_two.reshape(27, CH)
    core = lax.axis_index("core")
    parity = core.astype(jnp.int32).reshape(1)


    def both(x):
        return jnp.concatenate(
            [lax.dynamic_slice_in_dim(block, x, 1, 0) for block in (block_in, block_up)], axis=0
        )

    outer = both(core)
    outer, inner = lax.optimization_barrier((outer, 1 - core))
    far = with_other_chip(outer)
    near = with_other_core(both(inner))
    slots = pltpu.VMEM((4, PADDED, CH), bf16)
    local_w = pltpu.VMEM((6 * CH, 6 * CH), bf16)
    side_w = pltpu.VMEM((4 * CH, 6 * CH), bf16)
    flipped = pltpu.VMEM((3 * CH, CELLS), bf16)
    totals = pltpu.VMEM((3, CH, CH), f32)
    devices = math.prod(lax.axis_size(name) for name in ("dp", *SPACE))
    factor = 1.0 / math.sqrt(devices * 2 * CELLS)
    local_one, local_two, side_one, side_two, far_w1, far_w2 = call(
        taps_kernel,
        [],
        [shape((6 * CH, 6 * CH), bf16)] * 2 + [shape((4 * CH, 6 * CH), bf16)] * 4,
        1_000_000_000,
        parity, d1, point_one, d2, point_two,
    )
    inner, pre, carried, terms = call(
        functools.partial(near_kernel, factor),
        [slots, slots, flipped, flipped, totals],
        [shape((CELLS, CH), bf16)] + [shape((CELLS, CH), f32)] * 2 + [shape((TERMS, CH), f32)],
        6_000_000_000,
        parity, block_in, block_up, near, local_one, local_two, side_one, side_two,
        d1, point_one, d2, point_two,
    )
    outer, terms = call(
        functools.partial(far_kernel, factor),
        [slots, slots, flipped, flipped, totals],
        [shape((CELLS, CH), bf16), shape((TERMS, CH), f32)],
        4_000_000_000,
        parity, block_in, block_up, far, pre, carried, far_w1, far_w2,
        d1, point_one, d2, point_two, terms,
    )
    share = reduced_across(terms)
    outer_beside = with_other_chip(outer)
    inner_beside = with_other_core(inner)
    copies = reduced_around(share)
    copies, own_inner, own_outer = lax.optimization_barrier((copies, inner, outer))
    (own,) = call(
        own_kernel,
        [slots, local_w],
        [shape((2, CELLS, CH), f32)],
        8_000_000_000,
        parity, own_inner, own_outer, d1, point_one,
    )
    grad, done = call(
        last_kernel,
        [pltpu.VMEM((2, PADDED, CH), bf16), side_w, side_w],
        [shape((2, CELLS, CH), bf16), shape((8, CH), f32)],
        2_000_000_000,
        parity, own, inner_beside, outer_beside, d1, point_one,
    )
    sums = gathered_across(copies)
    depth, point = (shape((3, 3, 3, CH), f32), shape((CH, CH), f32))
    parts = call(parts_kernel, [], [depth, point, depth, point], 0, sums, done)
    return (grad.reshape(inputs.shape), *parts)


def solution(mesh):
    count, samples = (mesh.shape["space"], mesh.shape["dp"])
    ring = min(8, count // 2)
    grid = mesh.devices.reshape(count // (2 * ring), ring, 2, samples)
    split = jax.sharding.Mesh(grid, (*SPACE, "dp"))
    slabs = P("dp", SPACE, None, None, None, None)
    return jax.shard_map(
        on_device,
        mesh=split,
        in_specs=(slabs, P(), P(), P(), P(), slabs),
        out_specs=(slabs, P(), P(), P(), P()),
        check_vma=False,
    )
```

```python
import functools
import math

import jax
import jax.numpy as jnp
from jax import lax
from jax.experimental import pallas as pl
from jax.experimental.pallas import tpu as pltpu
from jax.sharding import PartitionSpec as P

CH = 128
LINE = 64
CELLS = 1024
PADDED = CELLS + 2 * LINE
ROWS = 512
TERMS = 320
VMEM_LIMIT = 24 * 1024 * 1024


def mm(a, b):
    return jnp.dot(a, b, preferred_element_type=jnp.float32)


def keep_mask(count, edge):
    return lax.broadcasted_iota(jnp.int32, (count, 1), 0) % LINE != edge


def from_before(v):
    return jnp.where(keep_mask(v.shape[0], 0), pltpu.roll(v, 1, 0), 0.0)


def from_after(v):
    return jnp.where(keep_mask(v.shape[0], LINE - 1), pltpu.roll(v, v.shape[0] - 1, 0), 0.0)


def shift_sum(products, width):
    return (
        from_before(products[:, :width])
        + products[:, width : 2 * width]
        + from_after(products[:, 2 * width :])
    )


def set_plane(ref, slot, plane):
    edge = jnp.zeros((LINE, CH), jnp.bfloat16)
    ref[slot, 0:LINE, :] = edge
    ref[slot, LINE : LINE + CELLS, :] = plane
    ref[slot, LINE + CELLS : PADDED, :] = edge


def local_products(planes, weights, start):
    left = jnp.concatenate(
        [
            planes[1 + p, start + b * LINE : start + b * LINE + ROWS, :]
            for p in range(2)
            for b in range(3)
        ],
        axis=1,
    )
    return shift_sum(mm(left, weights[...]), 2 * CH)


def side_products(planes, slot, weights, start):
    pairs = ROWS // LINE
    left = jnp.concatenate(
        [
            jnp.concatenate(
                [
                    planes[slot, start + (2 * j + i) * LINE : start + (2 * j + i + 1) * LINE, :]
                    for j in range(pairs)
                ],
                axis=0,
            )
            for i in range(4)
        ],
        axis=1,
    )
    out = shift_sum(mm(left, weights[...]), 2 * CH)
    return jnp.concatenate(
        [
            out[j * LINE : (j + 1) * LINE, q * CH : (q + 1) * CH]
            for j in range(pairs)
            for q in range(2)
        ],
        axis=0,
    )


def fill_local(ref, tap_matrix):
    for a in range(3):
        for b in range(3):
            for e in range(3):
                block = tap_matrix(9 * a + 3 * b + e)
                for p in range(2):
                    x = p + 1 - a
                    if 0 <= x < 2:
                        row, col = ((3 * p + b) * CH, (2 * e + x) * CH)
                        ref[row : row + CH, col : col + CH] = block


def fill_side(ref, tap_matrix, high):
    ref[...] = jnp.zeros(ref.shape, jnp.bfloat16)
    for b in range(3):
        for e in range(3):
            block = jnp.where(high, tap_matrix(18 + 3 * b + e), tap_matrix(3 * b + e))
            for q in range(2):
                row, col = ((b + q) * CH, (2 * e + q) * CH)
                ref[row : row + CH, col : col + CH] = block


def columns_of(depth):
    padded = jnp.concatenate([depth, jnp.zeros((CH - 27, CH), jnp.float32)], axis=0)
    return padded.T


def forward_taps(cols, point):
    return lambda s: (cols[:, s : s + 1] * point).astype(jnp.bfloat16)


def backward_taps(depth, point_t):
    return lambda s: (depth[26 - s : 27 - s, :] * point_t).astype(jnp.bfloat16)


def tap_sums(left_t, planes, x, combine):
    order = [(a, b) for a in range(3) for b in range(3)]
    for at in range(0, 9, 2):
        group = order[at : at + 2]
        right = jnp.concatenate(
            [planes[x + a, b * LINE : b * LINE + CELLS, :] for a, b in group], axis=1
        )
        sums = mm(left_t[...], right)
        for i, (a, b) in enumerate(group):
            for e in range(3):
                combine(9 * a + 3 * b + e, sums[e * CH : (e + 1) * CH, i * CH : (i + 1) * CH])


def activate(value, back, scaled_out, scaled_t, hidden_t, start):
    sigma = jax.nn.sigmoid(value)
    hidden = (value * sigma).astype(jnp.bfloat16).astype(jnp.float32)
    scaled = (back * (sigma * (1.0 + value * (1.0 - sigma)))).astype(jnp.bfloat16)
    scaled_out[start : start + ROWS, :] = scaled
    scaled = scaled.astype(jnp.float32)
    for ref, v in ((scaled_t, scaled), (hidden_t, hidden)):
        shifted = jnp.concatenate([from_after(v), v, from_before(v)], axis=1)
        ref[:, start : start + ROWS] = shifted.astype(jnp.bfloat16).T


def weight_terms(factor, x, planes_in, planes_up, scaled_t, hidden_t, weights, total, before, terms):
    depth_one, point_one, depth_two, point_two = weights
    point_one_t = point_one.T
    cols_two = columns_of(depth_two)
    lane = lax.broadcasted_iota(jnp.int32, (CH, CH), 1)
    total[...] = jnp.zeros((3, CH, CH), jnp.float32)
    terms[...] = jnp.zeros((TERMS, CH), jnp.float32) if before is None else before[...]

    def layer_one(s, block):
        total[0] += depth_one[s : s + 1, :] * block
        terms[s : s + 1, :] += jnp.sum(point_one_t * block, axis=0, keepdims=True) * factor

    tap_sums(scaled_t, planes_in, x, layer_one)
    terms[32:160, :] += total[0].T * factor

    def layer_two(s, block):
        s = 26 - s
        total[1] += cols_two[:, s : s + 1] * block
        total[2] += jnp.where(lane == s, jnp.sum(point_two * block, axis=1, keepdims=True), 0.0)

    tap_sums(hidden_t, planes_up, x, layer_two)
    terms[192:320, :] += total[1] * factor
    terms[160:192, :] += total[2].T[:32, :] * factor


def place_planes(planes, block, core, near, far):
    for x in range(2):
        set_plane(planes, 1 + x, block[x])
    if near is not None:
        set_plane(planes, 3 - 3 * core, near)
    if far is not None:
        set_plane(planes, 3 * core, far)


def taps_kernel(
    parity, d1, p1, d2, p2, local_one, local_two, side_one, side_two, far_w1, far_w2
):
    near_high = parity[0] == 0
    depth_one, point_one, depth_two, point_two = (
        w[...].astype(jnp.float32) for w in (d1, p1, d2, p2)
    )
    taps_one = forward_taps(columns_of(depth_one), point_one)
    taps_two = backward_taps(depth_two, point_two.T)
    for taps, local, side, other in (
        (taps_one, local_one, side_one, far_w1),
        (taps_two, local_two, side_two, far_w2),
    ):
        fill_local(local, taps)
        fill_side(side, taps, near_high)
        fill_side(other, taps, jnp.logical_not(near_high))


def near_kernel(
    factor,
    parity, block_in, block_up, near, local_one, local_two, side_one, side_two, d1, p1, d2, p2,
    scaled_out, pre, carried, terms,
    planes_in, planes_up, scaled_t, hidden_t, total,
):
    core = parity[0]
    inner = 1 - core
    weights = tuple(w[...].astype(jnp.float32) for w in (d1, p1, d2, p2))
    place_planes(planes_in, block_in, core, near[0], None)
    place_planes(planes_up, block_up, core, near[1], None)
    near_high = core == 0
    near_slot = 3 - 3 * core
    for half in range(0, CELLS, 2 * ROWS):
        side_in = side_products(planes_in, near_slot, side_one, half)
        side_up = side_products(planes_up, near_slot, side_two, half)
        for at in range(0, 2 * ROWS, ROWS):
            start = half + at
            both_in = local_products(planes_in, local_one, start)
            both_up = local_products(planes_up, local_two, start)
            low, high = (both_in[:, :CH], both_in[:, CH:])
            pre[start : start + ROWS, :] = jnp.where(near_high, low, high)
            value = jnp.where(near_high, high, low) + side_in[at : at + ROWS, :]
            low, high = (both_up[:, :CH], both_up[:, CH:])
            carried[start : start + ROWS, :] = jnp.where(near_high, low, high)
            back = jnp.where(near_high, high, low) + side_up[at : at + ROWS, :]
            activate(value, back, scaled_out, scaled_t, hidden_t, start)
    weight_terms(
        factor, inner, planes_in, planes_up, scaled_t, hidden_t, weights, total, None, terms
    )


def far_kernel(
    factor,
    parity, block_in, block_up, far, pre, carried, far_w1, far_w2, d1, p1, d2, p2, before,
    scaled_out, terms,
    planes_in, planes_up, scaled_t, hidden_t, total,
):
    core = parity[0]
    weights = tuple(w[...].astype(jnp.float32) for w in (d1, p1, d2, p2))
    place_planes(planes_in, block_in, core, None, far[0])
    place_planes(planes_up, block_up, core, None, far[1])
    for half in range(0, CELLS, 2 * ROWS):
        side_in = side_products(planes_in, 3 * core, far_w1, half)
        side_up = side_products(planes_up, 3 * core, far_w2, half)
        for at in range(0, 2 * ROWS, ROWS):
            start = half + at
            value = side_in[at : at + ROWS, :] + pre[start : start + ROWS, :]
            back = side_up[at : at + ROWS, :] + carried[start : start + ROWS, :]
            activate(value, back, scaled_out, scaled_t, hidden_t, start)
    weight_terms(
        factor, core, planes_in, planes_up, scaled_t, hidden_t, weights, total, before, terms
    )


def own_kernel(parity, inner, outer, d1, p1, out, planes, local):
    core = parity[0]
    depth_one = d1[...].astype(jnp.float32)
    fill_local(local, backward_taps(depth_one, p1[...].astype(jnp.float32).T))
    set_plane(planes, 2 - core, inner[...])
    set_plane(planes, 1 + core, outer[...])
    for start in range(0, CELLS, ROWS):
        both = local_products(planes, local, start)
        out[0, start : start + ROWS, :] = both[:, :CH]
        out[1, start : start + ROWS, :] = both[:, CH:]


def last_kernel(parity, own, near, far, d1, p1, out, done, planes, low_side, high_side):
    core = parity[0]
    depth_one = d1[...].astype(jnp.float32)
    taps = backward_taps(depth_one, p1[...].astype(jnp.float32).T)
    fill_side(low_side, taps, False)
    fill_side(high_side, taps, True)
    set_plane(planes, 1 - core, near[...])
    set_plane(planes, core, far[...])
    for start in range(0, CELLS, 2 * ROWS):
        rows = slice(start, start + 2 * ROWS)
        low = side_products(planes, 0, low_side, start)
        out[0, rows, :] = (own[0, rows, :] + low).astype(jnp.bfloat16)
        high = side_products(planes, 1, high_side, start)
        out[1, rows, :] = (own[1, rows, :] + high).astype(jnp.bfloat16)
    done[...] = jnp.zeros((8, CH), jnp.float32)


def sum_kernel(arrived, copies):
    total = arrived[0]
    for i in range(1, arrived.shape[0]):
        total = total + arrived[i]
    for i in range(copies.shape[0]):
        copies[i] = total


def parts_kernel(sums, done, depth_one, point_one, depth_two, point_two):
    for a in range(3):
        for b in range(3):
            row = 9 * a + 3 * b
            depth_one[a, b] = sums[row : row + 3, :]
            depth_two[a, b] = sums[160 + row : 163 + row, :]
    point_one[...] = sums[32:160, :]
    point_two[...] = sums[192:320, :]


def call(kernel, scratch, outs, flops, *args):
    vmem = pl.BlockSpec(memory_space=pltpu.VMEM)
    smem = pl.BlockSpec(memory_space=pltpu.SMEM)
    moved = sum(a.size * a.dtype.itemsize for a in args) + sum(
        o.size * o.dtype.itemsize for o in outs
    )
    return pl.pallas_call(
        kernel,
        out_shape=outs,
        in_specs=[smem if a.dtype == jnp.int32 else vmem for a in args],
        out_specs=[vmem] * len(outs),
        scratch_shapes=scratch,
        cost_estimate=pl.CostEstimate(flops=flops, bytes_accessed=moved, transcendentals=0),
        compiler_params=pltpu.CompilerParams(vmem_limit_bytes=VMEM_LIMIT),
    )(*args)


SPACE = ("outer", "ring", "core")
ACROSS = ("outer", "core", "dp")


def with_other_core(v):
    return lax.ppermute(v, "core", [(0, 1), (1, 0)])


def with_other_chip(v):
    count = math.prod(lax.axis_size(name) for name in SPACE)
    pairs = [(i, i + 1) for i in range(1, count - 1, 2)]
    return lax.ppermute(v, SPACE, pairs + [(j, i) for i, j in pairs])


def reduced_across(terms):
    count = math.prod(lax.axis_size(name) for name in ACROSS)
    tiles = terms.reshape(count, 1, -1)
    return lax.all_to_all(tiles, ACROSS, 0, 0, tiled=True).sum(axis=0)


def reduced_around(share):
    copies = jnp.broadcast_to(share, (lax.axis_size("ring"), *share.shape))
    arrived = lax.all_to_all(copies, "ring", 0, 0, tiled=True)
    count = math.prod(lax.axis_size(name) for name in ACROSS)
    (copies,) = call(
        sum_kernel, [], [jax.ShapeDtypeStruct((count, *share.shape), share.dtype)], 0, arrived
    )
    return copies


def gathered_across(copies):
    return lax.all_to_all(copies, ACROSS, 0, 0, tiled=True).reshape(TERMS, CH)


def on_device(inputs, depth_one, point_one, depth_two, point_two, cotangent):
    f32, bf16 = jnp.float32, jnp.bfloat16
    shape = jax.ShapeDtypeStruct
    block_in = inputs.reshape(2, CELLS, CH)
    block_up = cotangent.reshape(2, CELLS, CH)
    d1 = depth_one.reshape(27, CH)
    d2 = depth_two.reshape(27, CH)
    core = lax.axis_index("core")
    parity = core.astype(jnp.int32).reshape(1)


    def both(x):
        return jnp.concatenate(
            [lax.dynamic_slice_in_dim(block, x, 1, 0) for block in (block_in, block_up)], axis=0
        )

    outer = both(core)
    outer, inner = lax.optimization_barrier((outer, 1 - core))
    far = with_other_chip(outer)
    near = with_other_core(both(inner))
    slots = pltpu.VMEM((4, PADDED, CH), bf16)
    local_w = pltpu.VMEM((6 * CH, 6 * CH), bf16)
    side_w = pltpu.VMEM((4 * CH, 6 * CH), bf16)
    flipped = pltpu.VMEM((3 * CH, CELLS), bf16)
    totals = pltpu.VMEM((3, CH, CH), f32)
    devices = math.prod(lax.axis_size(name) for name in ("dp", *SPACE))
    factor = 1.0 / math.sqrt(devices * 2 * CELLS)
    local_one, local_two, side_one, side_two, far_w1, far_w2 = call(
        taps_kernel,
        [],
        [shape((6 * CH, 6 * CH), bf16)] * 2 + [shape((4 * CH, 6 * CH), bf16)] * 4,
        1_000_000_000,
        parity, d1, point_one, d2, point_two,
    )
    inner, pre, carried, terms = call(
        functools.partial(near_kernel, factor),
        [slots, slots, flipped, flipped, totals],
        [shape((CELLS, CH), bf16)] + [shape((CELLS, CH), f32)] * 2 + [shape((TERMS, CH), f32)],
        6_000_000_000,
        parity, block_in, block_up, near, local_one, local_two, side_one, side_two,
        d1, point_one, d2, point_two,
    )
    outer, terms = call(
        functools.partial(far_kernel, factor),
        [slots, slots, flipped, flipped, totals],
        [shape((CELLS, CH), bf16), shape((TERMS, CH), f32)],
        4_000_000_000,
        parity, block_in, block_up, far, pre, carried, far_w1, far_w2,
        d1, point_one, d2, point_two, terms,
    )
    share = reduced_across(terms)
    outer_beside = with_other_chip(outer)
    inner_beside = with_other_core(inner)
    copies = reduced_around(share)
    copies, own_inner, own_outer = lax.optimization_barrier((copies, inner, outer))
    (own,) = call(
        own_kernel,
        [slots, local_w],
        [shape((2, CELLS, CH), f32)],
        2_000_000_000,
        parity, own_inner, own_outer, d1, point_one,
    )
    grad, done = call(
        last_kernel,
        [pltpu.VMEM((2, PADDED, CH), bf16), side_w, side_w],
        [shape((2, CELLS, CH), bf16), shape((8, CH), f32)],
        2_000_000_000,
        parity, own, inner_beside, outer_beside, d1, point_one,
    )
    sums = gathered_across(copies)
    depth, point = (shape((3, 3, 3, CH), f32), shape((CH, CH), f32))
    parts = call(parts_kernel, [], [depth, point, depth, point], 0, sums, done)
    return (grad.reshape(inputs.shape), *parts)


def solution(mesh):
    count, samples = (mesh.shape["space"], mesh.shape["dp"])
    ring = min(8, count // 2)
    grid = mesh.devices.reshape(count // (2 * ring), ring, 2, samples)
    split = jax.sharding.Mesh(grid, (*SPACE, "dp"))
    slabs = P("dp", SPACE, None, None, None, None)
    return jax.shard_map(
        on_device,
        mesh=split,
        in_specs=(slabs, P(), P(), P(), P(), slabs),
        out_specs=(slabs, P(), P(), P(), P()),
        check_vma=False,
    )
```
